32 devices in a mesh: shard: 16 (over z, y, x), rep: 2 (over core).
Axes of the slice: x: 2, y: 2, z: 4, core: 2. Of those that a mesh axis runs over, the one named last changes fastest.
Arguments:
- momentum: bfloat16 [16, 512, 2048], P(None, 'shard'), may hold values from -6 to 6
- gradient: bfloat16 [16, 512, 2048], P(None, 'shard'), may hold values from -6 to 6
Outputs:
- new_momentum: bfloat16 [16, 512, 2048], P(None, 'shard')
- update: bfloat16 [16, 512, 2048], P(None, 'shard')
The draws below stay inside these ranges and needn't reach their ends.
All inputs are finite; a program needn't handle non-finite values.
Results may differ from the reference program's by a relative error of at most 0.00065.
The reference program's roundings to bfloat16 on the way (of `blended`) count: a program that leaves them out, or rounds other values in their place, can miss the bound.
Values may be sent and summed in bfloat16 or wider, within the bound.
No kernel may reach another device: no remote copies, remote signals or barrier semaphores. Data moves between devices by JAX's collectives and lax.ppermute only.
A program may use at most 64 MiB of HBM per device.

```python
import jax
import jax.numpy as jnp
from jax import lax

ROWS = 512
COLS = 2048
ITERS = 5
EXPERTS = 16


def shard_levels(own_key, extent, pieces, low, high):
    def one(axis_at, shards_of):
        draws = jax.random.uniform(jax.random.fold_in(jax.random.fold_in(own_key, 6), axis_at), (shards_of,), jnp.float32, low / len(pieces), high / len(pieces))
        return jnp.repeat(jnp.exp(draws), extent[axis_at] // shards_of).reshape((-1,) + (1,) * (len(extent) - axis_at - 1))

    factor_of = one(*pieces[0])
    for cut in pieces[1:]:
        factor_of = factor_of * one(*cut)
    return factor_of


def normal_values(key, dims, spread, limit, pieces=(), dtype=jnp.bfloat16):
    entries = jax.random.normal(key, dims, jnp.float32) * spread
    if len(pieces) > 0:
        entries = shard_levels(key, dims, pieces, -0.22, 0.18) * entries
    return jnp.clip(entries, min=-limit, max=limit).astype(dtype)


def setup_inputs(seed: int = 0) -> dict:
    keys = jax.random.split(jax.random.key(seed), 3)
    momentum = normal_values(keys[0], (EXPERTS, ROWS, COLS), 1.0, 6.0, ((1, 16),))
    gradient = normal_values(keys[1], (EXPERTS, ROWS, COLS), 1.0, 6.0, ((1, 16),))
    return {"momentum": momentum, "gradient": gradient}


coef_a = 3.4445
coef_b = -4.775
coef_c = 2.0315

def orthogonal(matrix):
    values = matrix.astype(jnp.float32)
    norm_value = jnp.sqrt(jnp.sum(values * values)) + 1e-07
    iterate = values / norm_value
    for sweep in range(ITERS):
        gram_matrix = jnp.dot(iterate, iterate.T, precision=lax.Precision.HIGHEST)
        polynomial = coef_b * gram_matrix + coef_c * jnp.dot(gram_matrix, gram_matrix, precision=lax.Precision.HIGHEST)
        iterate = coef_a * iterate + jnp.dot(polynomial, iterate, precision=lax.Precision.HIGHEST)
    return (iterate * jnp.sqrt(jnp.float32(max(ROWS, COLS)))).astype(jnp.bfloat16)

def reference(momentum, gradient):
    new_momentum = (0.95 * momentum.astype(jnp.float32) + gradient.astype(jnp.float32)).astype(jnp.bfloat16)
    blended = (gradient.astype(jnp.float32) + 0.95 * new_momentum.astype(jnp.float32)).astype(jnp.bfloat16)
    update = lax.map(orthogonal, blended)
    return (new_momentum, update)
```

```python
import functools

import jax
import jax.numpy as jnp
from jax import lax
from jax.experimental import pallas as pl
from jax.experimental.pallas import tpu as pltpu
from jax.sharding import PartitionSpec as P

ITERS = 5

coef_a = 3.4445
coef_b = -4.775
coef_c = 2.0315

BF = jnp.bfloat16
F32 = jnp.float32


def blend_kernel(rep_ref, m_ref, g_ref, new_ref, part_ref):
    width = part_ref.shape[-1]
    new_ref[...] = (0.95 * m_ref[...].astype(F32) + g_ref[...].astype(F32)).astype(BF)
    cols = pl.ds(pl.multiple_of(rep_ref[0] * width, width), width)
    part_ref[...] = (
        g_ref[:, :, cols].astype(F32) + 0.95 * new_ref[:, :, cols].astype(F32)
    ).astype(BF)


def blend(rep, momentum, gradient, n_rep):
    experts, rows, cols = momentum.shape
    step = 2
    whole = pl.BlockSpec((step, rows, cols), lambda i, r: (i, 0, 0))
    part = pl.BlockSpec((step, rows, cols // n_rep), lambda i, r: (i, 0, 0))
    return pl.pallas_call(
        blend_kernel,
        grid_spec=pltpu.PrefetchScalarGridSpec(
            num_scalar_prefetch=1,
            grid=(experts // step,),
            in_specs=[whole, whole],
            out_specs=[whole, part],
        ),
        out_shape=[
            jax.ShapeDtypeStruct(momentum.shape, BF),
            jax.ShapeDtypeStruct((experts, rows, cols // n_rep), BF),
        ],
        name="blend",
    )(rep, momentum, gradient)


def halves(x):
    high = x.astype(BF)
    return high, (x - high.astype(F32)).astype(BF)


def put_left(ref, x):
    n = x.shape[0]
    high, low = halves(x)
    ref[:, :n] = high
    ref[:, n : 2 * n] = high
    ref[:, 2 * n :] = low


def put_right(ref, x, at):
    n = x.shape[0]
    high, low = halves(x)
    ref[:n, at : at + n] = high
    ref[n : 2 * n, at : at + n] = low
    ref[2 * n :, at : at + n] = high


def dot(x, y):
    return jnp.dot(x, y, preferred_element_type=F32)


def orthogonal_kernel(scale, *refs):
    *parts, out_ref, a_ref, q_ref, s_ref, left, right = refs
    n = a_ref.shape[0]

    def gram(x):
        return lax.dot_general(
            x, x, (((1,), (1,)), ((), ())), preferred_element_type=F32
        )

    total = gram(parts[0][...])
    for part in parts[1:]:
        total = total + gram(part[...])
    eye = lax.broadcasted_iota(jnp.int32, (n, n), 0) == lax.broadcasted_iota(
        jnp.int32, (n, n), 1
    )
    square = jnp.sum(jnp.where(eye, total, 0.0), keepdims=True)
    inverse = 1.0 / (jnp.sqrt(square) + 1e-07)
    first = total * (inverse * inverse)
    a_ref[...] = first

    def middle():
        a = a_ref[...]
        put_left(left, a)
        put_right(right, a, 0)
        m = coef_b * a + coef_c * dot(left[...], right[:, :n])
        put_left(left, m)
        return m

    def advance():
        s_ref[...] = coef_a * a_ref[...] + dot(left[...], right[:, :n])
        put_right(right, s_ref[...], 0)
        a_ref[...] = coef_a * s_ref[...] + dot(left[...], right[:, :n])

    q_ref[...] = jnp.where(eye, coef_a, 0.0) + middle()
    advance()

    def step(_, carry):
        middle()
        put_right(right, q_ref[...], n)
        q_ref[...] = coef_a * q_ref[...] + dot(left[...], right[:, n:])
        advance()
        return carry

    lax.fori_loop(1, ITERS - 1, step, 0)
    middle()
    put_right(right, q_ref[...], n)
    q = coef_a * q_ref[...] + dot(left[...], right[:, n:])
    high, low = halves(q * (inverse * scale))
    left[:, :n] = high
    left[:, n : 2 * n] = low
    width = out_ref.shape[1]
    block = min(width, 256)
    for at in range(0, width, block):
        x = parts[0][:, at : at + block]
        out_ref[:, at : at + block] = (
            dot(left[:, :n], x) + dot(left[:, n : 2 * n], x)
        ).astype(BF)


def orthogonal(parts, scale):
    rows, width = parts[0].shape
    vmem = pl.BlockSpec(memory_space=pltpu.VMEM)
    return pl.pallas_call(
        functools.partial(orthogonal_kernel, scale),
        in_specs=[vmem] * len(parts),
        out_specs=vmem,
        out_shape=jax.ShapeDtypeStruct((rows, width), BF),
        scratch_shapes=[
            pltpu.VMEM((rows, rows), F32),
            pltpu.VMEM((rows, rows), F32),
            pltpu.VMEM((rows, rows), F32),
            pltpu.VMEM((rows, 3 * rows), BF),
            pltpu.VMEM((3 * rows, 2 * rows), BF),
        ],
        compiler_params=pltpu.CompilerParams(vmem_limit_bytes=40 * 2**20),
        name="orthogonal",
    )(*parts)


def solution(mesh):
    n_rep = mesh.shape["rep"]

    def swap(x):
        return [
            lax.ppermute(x, "rep", [((i + j) % n_rep, i) for i in range(n_rep)])
            for j in range(1, n_rep)
        ]

    def shards(momentum, gradient):
        experts, rows, cols = momentum.shape
        rep = lax.axis_index("rep")
        new_momentum, part = blend(rep[None], momentum, gradient, n_rep)
        width = part.shape[2]
        mine = lax.all_to_all(part, "shard", split_axis=0, concat_axis=0, tiled=True)
        mine = mine.reshape(experts * rows, width)
        scale = float(max(experts * rows, cols)) ** 0.5
        update = orthogonal([mine, *swap(mine)], scale)
        update = lax.all_to_all(
            update.reshape(experts, rows, width), "shard", split_axis=0, concat_axis=0, tiled=True
        )
        whole = jnp.zeros((experts, rows, cols), BF)
        for j, piece in enumerate([update, *swap(update)]):
            at = lax.rem(rep + j, n_rep) * width
            whole = lax.dynamic_update_slice(whole, piece, (0, 0, at))
        return new_momentum, whole

    return jax.shard_map(
        shards,
        mesh=mesh,
        in_specs=(P(None, "shard", None), P(None, "shard", None)),
        out_specs=(P(None, "shard", None), P(None, "shard", None)),
        check_vma=False,
    )
```

```python
import functools

import jax
import jax.numpy as jnp
from jax import lax
from jax.experimental import pallas as pl
from jax.experimental.pallas import tpu as pltpu
from jax.sharding import PartitionSpec as P

ITERS = 5

coef_a = 3.4445
coef_b = -4.775
coef_c = 2.0315

BF = jnp.bfloat16
F32 = jnp.float32


def pieces_kernel(at_ref, m_ref, g_ref, *part_refs):
    experts = len(part_refs)
    for k, part_ref in enumerate(part_refs):
        e = lax.rem(at_ref[0] + k, experts)
        g = g_ref[e].astype(F32)
        new = (0.95 * m_ref[e].astype(F32) + g).astype(BF)
        part_ref[...] = (g + 0.95 * new.astype(F32)).astype(BF)


def blended_pieces(at, momentum, gradient, n_rep):
    experts, rows, cols = momentum.shape
    width = cols // n_rep
    block = pl.BlockSpec((experts, rows, width), lambda i, at: (0, 0, at[1]))
    piece = pl.BlockSpec((rows, width), lambda i, at: (0, 0))
    return pl.pallas_call(
        pieces_kernel,
        grid_spec=pltpu.PrefetchScalarGridSpec(
            num_scalar_prefetch=1,
            grid=(1,),
            in_specs=[block, block],
            out_specs=[piece] * experts,
        ),
        out_shape=[jax.ShapeDtypeStruct((rows, width), BF)] * experts,
        compiler_params=pltpu.CompilerParams(vmem_limit_bytes=24 * 2**20),
        name="blended",
    )(at, momentum, gradient)


def momentum_kernel(m_ref, g_ref, new_ref):
    new_ref[...] = (0.95 * m_ref[...].astype(F32) + g_ref[...].astype(F32)).astype(BF)


def next_momentum(momentum, gradient):
    experts, rows, cols = momentum.shape
    step = 2
    block = pl.BlockSpec((step, rows, cols), lambda i: (i, 0, 0))
    return pl.pallas_call(
        momentum_kernel,
        grid=(experts // step,),
        in_specs=[block, block],
        out_specs=block,
        out_shape=jax.ShapeDtypeStruct(momentum.shape, BF),
        cost_estimate=pl.CostEstimate(
            flops=2 * momentum.size, bytes_accessed=6 * momentum.size, transcendentals=0
        ),
        name="new_momentum",
    )(momentum, gradient)


def halves(x):
    high = x.astype(BF)
    return high, (x - high.astype(F32)).astype(BF)


def put_left(ref, x):
    n = x.shape[0]
    high, low = halves(x)
    ref[:, :n] = high
    ref[:, n : 2 * n] = high
    ref[:, 2 * n :] = low


def put_right(ref, x, at):
    n = x.shape[0]
    high, low = halves(x)
    ref[:n, at : at + n] = high
    ref[n : 2 * n, at : at + n] = low
    ref[2 * n :, at : at + n] = high


def dot(x, y):
    return jnp.dot(x, y, preferred_element_type=F32)


def orthogonal_kernel(scale, count, n_in, *refs):
    ins, refs = refs[:n_in], refs[n_in:]
    out_refs, (a_ref, q_ref, s_ref, left, right, *parts) = refs[:count], refs[count:]
    n = a_ref.shape[0]
    rows, width = ins[0].shape
    for i, ref in enumerate(ins):
        at = i % count * rows
        parts[i // count][at : at + rows, :] = ref[...]

    def gram(x):
        return lax.dot_general(
            x, x, (((1,), (1,)), ((), ())), preferred_element_type=F32
        )

    total = gram(parts[0][...])
    for part in parts[1:]:
        total = total + gram(part[...])
    eye = lax.broadcasted_iota(jnp.int32, (n, n), 0) == lax.broadcasted_iota(
        jnp.int32, (n, n), 1
    )
    square = jnp.sum(jnp.where(eye, total, 0.0), keepdims=True)
    inverse = 1.0 / (jnp.sqrt(square) + 1e-07)
    first = total * (inverse * inverse)
    a_ref[...] = first

    def middle():
        a = a_ref[...]
        put_left(left, a)
        put_right(right, a, 0)
        m = coef_b * a + coef_c * dot(left[...], right[:, :n])
        put_left(left, m)
        return m

    def advance():
        s_ref[...] = coef_a * a_ref[...] + dot(left[...], right[:, :n])
        put_right(right, s_ref[...], 0)
        a_ref[...] = coef_a * s_ref[...] + dot(left[...], right[:, :n])

    q_ref[...] = jnp.where(eye, coef_a, 0.0) + middle()
    advance()

    def step(_, carry):
        middle()
        put_right(right, q_ref[...], n)
        q_ref[...] = coef_a * q_ref[...] + dot(left[...], right[:, n:])
        advance()
        return carry

    lax.fori_loop(1, ITERS - 1, step, 0)
    middle()
    put_right(right, q_ref[...], n)
    q = coef_a * q_ref[...] + dot(left[...], right[:, n:])
    high, low = halves(q * (inverse * scale))
    left[:, :n] = high
    left[:, n : 2 * n] = low
    block = min(width, 256)
    for at in range(0, width, block):
        x = parts[0][:, at : at + block]
        y = (dot(left[:, :n], x) + dot(left[:, n : 2 * n], x)).astype(BF)
        for i, out_ref in enumerate(out_refs):
            out_ref[:, at : at + block] = y[i * rows : (i + 1) * rows]


def orthogonal(parts, scale):
    count = len(parts[0])
    rows, width = parts[0][0].shape
    n = rows * count
    flat = [piece for part in parts for piece in part]
    vmem = pl.BlockSpec(memory_space=pltpu.VMEM)
    return pl.pallas_call(
        functools.partial(orthogonal_kernel, scale, count, len(flat)),
        in_specs=[vmem] * len(flat),
        out_specs=[vmem] * count,
        out_shape=[jax.ShapeDtypeStruct((rows, width), BF)] * count,
        scratch_shapes=[
            pltpu.VMEM((n, n), F32),
            pltpu.VMEM((n, n), F32),
            pltpu.VMEM((n, n), F32),
            pltpu.VMEM((n, 3 * n), BF),
            pltpu.VMEM((3 * n, 2 * n), BF),
        ]
        + [pltpu.VMEM((n, width), BF)] * len(parts),
        compiler_params=pltpu.CompilerParams(vmem_limit_bytes=40 * 2**20),
        name="orthogonal",
    )(*flat)


def collect_kernel(count, at_ref, *refs):
    *ins, out_ref = refs
    width = ins[0].shape[1]
    n_rep = len(ins) // count
    for i, ref in enumerate(ins):
        e = lax.rem(at_ref[0] + i % count, count)
        c = lax.rem(at_ref[1] + i // count, n_rep)
        out_ref[e, :, pl.ds(pl.multiple_of(c * width, width), width)] = ref[...]


def collect(at, parts):
    count = len(parts[0])
    rows, width = parts[0][0].shape
    flat = [piece for part in parts for piece in part]
    shape = (count, rows, width * len(parts))
    piece = pl.BlockSpec((rows, width), lambda i, at: (0, 0))
    return pl.pallas_call(
        functools.partial(collect_kernel, count),
        grid_spec=pltpu.PrefetchScalarGridSpec(
            num_scalar_prefetch=1,
            grid=(1,),
            in_specs=[piece] * len(flat),
            out_specs=pl.BlockSpec(shape, lambda i, at: (0, 0, 0)),
        ),
        out_shape=jax.ShapeDtypeStruct(shape, BF),
        compiler_params=pltpu.CompilerParams(vmem_limit_bytes=24 * 2**20),
        name="collect",
    )(at, *flat)


def solution(mesh):
    n_rep = mesh.shape["rep"]
    n_shard = mesh.shape["shard"]

    def turn(x, axis, size, j):
        return lax.ppermute(x, axis, [(i, (i + j) % size) for i in range(size)])

    def others(pieces):
        if n_rep == 2:
            return [[turn(x, "rep", n_rep, 1) for x in pieces]]
        whole = jnp.concatenate(pieces)
        return [
            jnp.split(turn(whole, "rep", n_rep, -j), len(pieces)) for j in range(1, n_rep)
        ]

    def shards(momentum, gradient):
        experts, rows, cols = momentum.shape
        at = jnp.stack([lax.axis_index("shard"), lax.axis_index("rep")])
        sent = blended_pieces(at, momentum, gradient, n_rep)
        mine = [turn(x, "shard", n_shard, k) if k else x for k, x in enumerate(sent)]
        new_momentum = next_momentum(momentum, gradient)
        scale = float(max(experts * rows, cols)) ** 0.5
        update = orthogonal([mine, *others(mine)], scale)
        update = [turn(x, "shard", n_shard, -k) if k else x for k, x in enumerate(update)]
        return new_momentum, collect(at, [update, *others(update)])

    return jax.shard_map(
        shards,
        mesh=mesh,
        in_specs=(P(None, "shard", None), P(None, "shard", None)),
        out_specs=(P(None, "shard", None), P(None, "shard", None)),
        check_vma=False,
    )
```

```python
import functools

import jax
import jax.numpy as jnp
from jax import lax
from jax.experimental import pallas as pl
from jax.experimental.pallas import tpu as pltpu
from jax.sharding import PartitionSpec as P

ITERS = 5

coef_a = 3.4445
coef_b = -4.775
coef_c = 2.0315

BF = jnp.bfloat16
F32 = jnp.float32


def next_momentum(m, g):
    return (0.95 * m.astype(F32) + g.astype(F32)).astype(BF)


def blend(m, g):
    return (g.astype(F32) + 0.95 * next_momentum(m, g).astype(F32)).astype(BF)


def share_kernel(rep_ref, m_hbm, g_hbm, share_ref, m_ref, g_ref, sems):
    experts, height, _ = share_ref.shape
    chunks = sems.shape[1]
    step = experts // chunks
    rows = pl.ds(pl.multiple_of(rep_ref[0] * height, height), height)
    copies = []
    for i in range(chunks):
        at = pl.ds(i * step, step)
        copies.append(
            [
                pltpu.make_async_copy(src.at[at, rows], dst.at[at], sems.at[j, i])
                for j, (src, dst) in enumerate(((m_hbm, m_ref), (g_hbm, g_ref)))
            ]
        )
        for copy in copies[-1]:
            copy.start()
    for i in range(chunks):
        for copy in copies[i]:
            copy.wait()
        at = slice(i * step, (i + 1) * step)
        share_ref[at] = blend(m_ref[at], g_ref[at])


def blended_share(rep, momentum, gradient, n_rep):
    experts, rows, cols = momentum.shape
    height = rows // n_rep
    shape = (experts, height, cols)
    if height % 16:
        m, g = (
            lax.dynamic_slice_in_dim(x, rep * height, height, 1) for x in (momentum, gradient)
        )
        return blend(m, g)
    chunks = 4 if experts % 4 == 0 else 1
    hbm = pl.BlockSpec(memory_space=pltpu.HBM)
    return pl.pallas_call(
        share_kernel,
        in_specs=[pl.BlockSpec(memory_space=pltpu.SMEM), hbm, hbm],
        out_specs=pl.BlockSpec(memory_space=pltpu.VMEM),
        out_shape=jax.ShapeDtypeStruct(shape, BF),
        scratch_shapes=[
            pltpu.VMEM(shape, BF),
            pltpu.VMEM(shape, BF),
            pltpu.SemaphoreType.DMA((2, chunks)),
        ],
        compiler_params=pltpu.CompilerParams(vmem_limit_bytes=16 * 2**20),
        name="share",
    )(rep[None], momentum, gradient)


def momentum_kernel(m_ref, g_ref, new_ref):
    def one(e, carry):
        new_ref[e] = next_momentum(m_ref[e], g_ref[e])
        return carry

    lax.fori_loop(0, m_ref.shape[0], one, 0)


def new_momentum_of(momentum, gradient):
    vmem = pl.BlockSpec(memory_space=pltpu.VMEM)
    return pl.pallas_call(
        momentum_kernel,
        in_specs=[vmem, vmem],
        out_specs=vmem,
        out_shape=jax.ShapeDtypeStruct(momentum.shape, BF),
        cost_estimate=pl.CostEstimate(
            flops=2 * momentum.size, bytes_accessed=6 * momentum.size, transcendentals=0
        ),
        compiler_params=pltpu.CompilerParams(vmem_limit_bytes=16 * 2**20),
        name="new_momentum",
    )(momentum, gradient)


def halves(x):
    high = x.astype(BF)
    return high, (x - high.astype(F32)).astype(BF)


def put_left(ref, x):
    rows, n = x.shape
    high, low = halves(x)
    ref[:rows, :n] = high
    ref[:rows, n : 2 * n] = high
    ref[:rows, 2 * n :] = low


def put_right(ref, x):
    n = x.shape[0]
    high, low = halves(x)
    ref[:n] = high
    ref[n : 2 * n] = low
    ref[2 * n :] = high


def dot(x, y):
    return jnp.dot(x, y, preferred_element_type=F32)


def dot_transposed(x, y):
    return lax.dot_general(x, y, (((1,), (1,)), ((), ())), preferred_element_type=F32)


def put_symmetric(ref, upper, corner):
    half = corner.shape[0]
    ref[:half] = upper
    ref[half:, half:] = corner
    ref[half:, :half] = upper[:, half:].T


def orthogonal_kernel(scale, *refs):
    *parts, out_ref, x_ref, a_ref, s_ref, y_ref, q_ref, left, right = refs
    height = out_ref.shape[0]
    n = x_ref.shape[0]
    half = n // 2
    for i, part in enumerate(parts):
        x_ref[i * height : (i + 1) * height] = part[...]

    put_symmetric(
        y_ref,
        dot_transposed(x_ref[:half], x_ref[...]),
        dot_transposed(x_ref[half:], x_ref[half:]),
    )
    eye = lax.broadcasted_iota(jnp.int32, (n, n), 0) == lax.broadcasted_iota(
        jnp.int32, (n, n), 1
    )
    square = jnp.sum(jnp.where(eye, y_ref[...], 0.0), keepdims=True)
    inverse = 1.0 / (jnp.sqrt(square) + 1e-07)
    a_ref[...] = y_ref[...] * (inverse * inverse)

    def multiply(ref):
        put_symmetric(
            ref, dot(left[:half], right[...]), dot(left[half:], right[:, half:])
        )

    def middle():
        a = a_ref[...]
        put_left(left, a)
        put_right(right, a)
        multiply(y_ref)
        m = coef_b * a + coef_c * y_ref[...]
        put_right(right, m)
        return m

    def advance():
        multiply(y_ref)
        s = coef_a * a_ref[...] + y_ref[...]
        s_ref[...] = s
        put_left(left, s)
        multiply(y_ref)
        a_ref[...] = coef_a * s_ref[...] + y_ref[...]

    def extend():
        put_left(left, q_ref[...])
        return coef_a * q_ref[...] + dot(left[:height], right[...])

    q_ref[...] = jnp.where(eye[:height], coef_a, 0.0) + middle()[:height]
    advance()

    def step(_, carry):
        middle()
        advance()
        q_ref[...] = extend()
        return carry

    lax.fori_loop(1, ITERS - 1, step, 0)
    middle()
    high, low = halves(extend() * (inverse * scale))
    left[:height, :n] = high
    left[:height, n : 2 * n] = low
    width = out_ref.shape[1]
    block = min(width, 512)
    for at in range(0, width, block):
        x = x_ref[:, at : at + block]
        out_ref[:, at : at + block] = (
            dot(left[:height, :n], x) + dot(left[:height, n : 2 * n], x)
        ).astype(BF)


def orthogonal(parts, scale):
    height, cols = parts[0].shape
    n = height * len(parts)
    vmem = pl.BlockSpec(memory_space=pltpu.VMEM)
    return pl.pallas_call(
        functools.partial(orthogonal_kernel, scale),
        in_specs=[vmem] * len(parts),
        out_specs=vmem,
        out_shape=jax.ShapeDtypeStruct((height, cols), BF),
        scratch_shapes=[
            pltpu.VMEM((n, cols), BF),
            pltpu.VMEM((n, n), F32),
            pltpu.VMEM((n, n), F32),
            pltpu.VMEM((n, n), F32),
            pltpu.VMEM((height, n), F32),
            pltpu.VMEM((n, 3 * n), BF),
            pltpu.VMEM((3 * n, n), BF),
        ],
        compiler_params=pltpu.CompilerParams(vmem_limit_bytes=40 * 2**20),
        name="orthogonal",
    )(*parts)


def place_kernel(rep_ref, part_ref, *refs):
    *_, out_ref, sem = refs
    height = part_ref.shape[1]
    rows = pl.ds(pl.multiple_of(rep_ref[0] * height, height), height)
    copy = pltpu.make_async_copy(part_ref, out_ref.at[:, rows], sem)
    copy.start()
    copy.wait()


def place(which, part, whole):
    experts, height, cols = part.shape
    if height % 16:
        if isinstance(whole, tuple):
            whole = jnp.zeros(whole, BF)
        return lax.dynamic_update_slice(whole, part, (0, which * height, 0))
    anywhere = pl.BlockSpec(memory_space=pl.ANY)
    hbm = pl.BlockSpec(memory_space=pltpu.HBM)
    first = isinstance(whole, tuple)
    return pl.pallas_call(
        place_kernel,
        in_specs=[pl.BlockSpec(memory_space=pltpu.SMEM), anywhere] + [hbm] * (not first),
        out_specs=hbm,
        out_shape=jax.ShapeDtypeStruct(whole if first else whole.shape, BF),
        scratch_shapes=[pltpu.SemaphoreType.DMA(())],
        input_output_aliases={} if first else {2: 0},
        cost_estimate=pl.CostEstimate(
            flops=0, bytes_accessed=4 * part.size, transcendentals=0
        ),
        compiler_params=pltpu.CompilerParams(vmem_limit_bytes=4 * 2**20),
        name="place",
    )(which[None], part, *([] if first else [whole]))


def solution(mesh):
    n_rep = mesh.shape["rep"]

    def others(x):
        return [
            lax.ppermute(x, "rep", [((i + j) % n_rep, i) for i in range(n_rep)])
            for j in range(1, n_rep)
        ]

    def exchange(x):
        return lax.all_to_all(x, "shard", split_axis=0, concat_axis=0, tiled=True)

    def shards(momentum, gradient):
        experts, rows, cols = momentum.shape
        rep = lax.axis_index("rep")
        share = exchange(blended_share(rep, momentum, gradient, n_rep))
        own = share.reshape(-1, cols)
        rest = others(own)
        momentum, gradient, own = lax.optimization_barrier((momentum, gradient, own))
        new_momentum = new_momentum_of(momentum, gradient)
        rest, new_momentum = lax.optimization_barrier((rest, new_momentum))
        scale = float(max(experts * rows, cols)) ** 0.5
        update = exchange(orthogonal([own, *rest], scale).reshape(share.shape))
        whole = (experts, rows, cols)
        for j, part in enumerate([update, *others(update)]):
            whole = place(lax.rem(rep + j, n_rep), part, whole)
        return new_momentum, whole

    return jax.shard_map(
        shards,
        mesh=mesh,
        in_specs=(P(None, "shard", None), P(None, "shard", None)),
        out_specs=(P(None, "shard", None), P(None, "shard", None)),
        check_vma=False,
    )
```

```python
import functools

import jax
import jax.numpy as jnp
from jax import lax
from jax.experimental import pallas as pl
from jax.experimental.pallas import tpu as pltpu
from jax.sharding import PartitionSpec as P

ITERS = 5

coef_a = 3.4445
coef_b = -4.775
coef_c = 2.0315

BF = jnp.bfloat16
F32 = jnp.float32


def next_momentum(m, g):
    return (0.95 * m.astype(F32) + g.astype(F32)).astype(BF)


def blend(m, g):
    return (g.astype(F32) + 0.95 * next_momentum(m, g).astype(F32)).astype(BF)


def share_kernel(rep_ref, m_hbm, g_hbm, share_ref, m_ref, g_ref, sems):
    experts, height, _ = share_ref.shape
    chunks = sems.shape[1]
    step = experts // chunks
    rows = pl.ds(pl.multiple_of(rep_ref[0] * height, height), height)
    copies = []
    for i in range(chunks):
        at = pl.ds(i * step, step)
        copies.append(
            [
                pltpu.make_async_copy(src.at[at, rows], dst.at[at], sems.at[j, i])
                for j, (src, dst) in enumerate(((m_hbm, m_ref), (g_hbm, g_ref)))
            ]
        )
        for copy in copies[-1]:
            copy.start()
    for i in range(chunks):
        for copy in copies[i]:
            copy.wait()
        at = slice(i * step, (i + 1) * step)
        share_ref[at] = blend(m_ref[at], g_ref[at])


def blended_share(rep, momentum, gradient, n_rep):
    experts, rows, cols = momentum.shape
    height = rows // n_rep
    shape = (experts, height, cols)
    if height % 16:
        m, g = (
            lax.dynamic_slice_in_dim(x, rep * height, height, 1) for x in (momentum, gradient)
        )
        return blend(m, g)
    chunks = 4 if experts % 4 == 0 else 1
    hbm = pl.BlockSpec(memory_space=pltpu.HBM)
    return pl.pallas_call(
        share_kernel,
        in_specs=[pl.BlockSpec(memory_space=pltpu.SMEM), hbm, hbm],
        out_specs=pl.BlockSpec(memory_space=pltpu.VMEM),
        out_shape=jax.ShapeDtypeStruct(shape, BF),
        scratch_shapes=[
            pltpu.VMEM(shape, BF),
            pltpu.VMEM(shape, BF),
            pltpu.SemaphoreType.DMA((2, chunks)),
        ],
        compiler_params=pltpu.CompilerParams(vmem_limit_bytes=60 * 2**20),
        name="share",
    )(rep[None], momentum, gradient)


def momentum_kernel(m_ref, g_ref, new_ref):
    def one(e, carry):
        new_ref[e] = next_momentum(m_ref[e], g_ref[e])
        return carry

    lax.fori_loop(0, m_ref.shape[0], one, 0)


def new_momentum_of(momentum, gradient):
    vmem = pl.BlockSpec(memory_space=pltpu.VMEM)
    return pl.pallas_call(
        momentum_kernel,
        in_specs=[vmem, vmem],
        out_specs=vmem,
        out_shape=jax.ShapeDtypeStruct(momentum.shape, BF),
        cost_estimate=pl.CostEstimate(
            flops=2 * momentum.size, bytes_accessed=6 * momentum.size, transcendentals=0
        ),
        compiler_params=pltpu.CompilerParams(vmem_limit_bytes=16 * 2**20),
        name="new_momentum",
    )(momentum, gradient)


def halves(x):
    high = x.astype(BF)
    return high, (x - high.astype(F32)).astype(BF)


def put_left(ref, x):
    rows, n = x.shape
    high, low = halves(x)
    ref[:rows, :n] = high
    ref[:rows, n : 2 * n] = high
    ref[:rows, 2 * n :] = low


def put_right(ref, x):
    n = x.shape[0]
    high, low = halves(x)
    ref[:n] = high
    ref[n : 2 * n] = low
    ref[2 * n :] = high


def dot(x, y):
    return jnp.dot(x, y, preferred_element_type=F32)


def dot_transposed(x, y):
    return lax.dot_general(x, y, (((1,), (1,)), ((), ())), preferred_element_type=F32)


def put_symmetric(ref, upper, corner):
    half = corner.shape[0]
    ref[:half] = upper
    ref[half:, half:] = corner
    ref[half:, :half] = upper[:, half:].T


def orthogonal_kernel(scale, *refs):
    *parts, out_ref, x_ref, a_ref, s_ref, y_ref, q_ref, left, right = refs
    height = out_ref.shape[0]
    n = x_ref.shape[0]
    half = n // 2
    for i, part in enumerate(parts):
        x_ref[i * height : (i + 1) * height] = part[...]

    put_symmetric(
        y_ref,
        dot_transposed(x_ref[:half], x_ref[...]),
        dot_transposed(x_ref[half:], x_ref[half:]),
    )
    eye = lax.broadcasted_iota(jnp.int32, (n, n), 0) == lax.broadcasted_iota(
        jnp.int32, (n, n), 1
    )
    square = jnp.sum(jnp.where(eye, y_ref[...], 0.0), keepdims=True)
    inverse = 1.0 / (jnp.sqrt(square) + 1e-07)
    a_ref[...] = y_ref[...] * (inverse * inverse)

    def multiply(ref):
        put_symmetric(
            ref, dot(left[:half], right[...]), dot(left[half:], right[:, half:])
        )

    def middle():
        a = a_ref[...]
        put_left(left, a)
        put_right(right, a)
        multiply(y_ref)
        m = coef_b * a + coef_c * y_ref[...]
        put_right(right, m)
        return m

    def advance():
        multiply(y_ref)
        s = coef_a * a_ref[...] + y_ref[...]
        s_ref[...] = s
        put_left(left, s)
        multiply(y_ref)
        a_ref[...] = coef_a * s_ref[...] + y_ref[...]

    def extend():
        put_left(left, q_ref[...])
        return coef_a * q_ref[...] + dot(left[:height], right[...])

    q_ref[...] = jnp.where(eye[:height], coef_a, 0.0) + middle()[:height]
    advance()

    def step(_, carry):
        middle()
        advance()
        q_ref[...] = extend()
        return carry

    lax.fori_loop(1, ITERS - 1, step, 0)
    middle()
    high, low = halves(extend() * (inverse * scale))
    left[:height, :n] = high
    left[:height, n : 2 * n] = low
    width = out_ref.shape[1]
    block = min(width, 512)
    for at in range(0, width, block):
        x = x_ref[:, at : at + block]
        out_ref[:, at : at + block] = (
            dot(left[:height, :n], x) + dot(left[:height, n : 2 * n], x)
        ).astype(BF)


def orthogonal(parts, scale):
    height, cols = parts[0].shape
    n = height * len(parts)
    vmem = pl.BlockSpec(memory_space=pltpu.VMEM)
    return pl.pallas_call(
        functools.partial(orthogonal_kernel, scale),
        in_specs=[vmem] * len(parts),
        out_specs=vmem,
        out_shape=jax.ShapeDtypeStruct((height, cols), BF),
        scratch_shapes=[
            pltpu.VMEM((n, cols), BF),
            pltpu.VMEM((n, n), F32),
            pltpu.VMEM((n, n), F32),
            pltpu.VMEM((n, n), F32),
            pltpu.VMEM((height, n), F32),
            pltpu.VMEM((n, 3 * n), BF),
            pltpu.VMEM((3 * n, n), BF),
        ],
        compiler_params=pltpu.CompilerParams(vmem_limit_bytes=40 * 2**20),
        name="orthogonal",
    )(*parts)


def place_kernel(rep_ref, part_ref, *refs):
    *_, out_ref, sem = refs
    height = part_ref.shape[1]
    rows = pl.ds(pl.multiple_of(rep_ref[0] * height, height), height)
    copy = pltpu.make_async_copy(part_ref, out_ref.at[:, rows], sem)
    copy.start()
    copy.wait()


def place(which, part, whole):
    experts, height, cols = part.shape
    if height % 16:
        if isinstance(whole, tuple):
            whole = jnp.zeros(whole, BF)
        return lax.dynamic_update_slice(whole, part, (0, which * height, 0))
    anywhere = pl.BlockSpec(memory_space=pl.ANY)
    hbm = pl.BlockSpec(memory_space=pltpu.HBM)
    first = isinstance(whole, tuple)
    return pl.pallas_call(
        place_kernel,
        in_specs=[pl.BlockSpec(memory_space=pltpu.SMEM), anywhere] + [hbm] * (not first),
        out_specs=hbm,
        out_shape=jax.ShapeDtypeStruct(whole if first else whole.shape, BF),
        scratch_shapes=[pltpu.SemaphoreType.DMA(())],
        input_output_aliases={} if first else {2: 0},
        cost_estimate=pl.CostEstimate(
            flops=0, bytes_accessed=4 * part.size, transcendentals=0
        ),
        compiler_params=pltpu.CompilerParams(vmem_limit_bytes=4 * 2**20),
        name="place",
    )(which[None], part, *([] if first else [whole]))


def solution(mesh):
    n_rep = mesh.shape["rep"]
    n_shard = mesh.shape["shard"]
    order = [p // 2 + p % 2 * (n_shard // 2) if n_shard % 2 == 0 else p for p in range(n_shard)]

    def others(x):
        return [
            lax.ppermute(x, "rep", [((i + j) % n_rep, i) for i in range(n_rep)])
            for j in range(1, n_rep)
        ]

    def exchange(x):
        return lax.all_to_all(
            x, "shard", split_axis=0, concat_axis=0, axis_index_groups=[order], tiled=True
        )

    def shards(momentum, gradient):
        experts, rows, cols = momentum.shape
        rep = lax.axis_index("rep")
        share = exchange(blended_share(rep, momentum, gradient, n_rep))
        own = share.reshape(-1, cols)
        rest = others(own)
        momentum, gradient, own = lax.optimization_barrier((momentum, gradient, own))
        new_momentum = new_momentum_of(momentum, gradient)
        rest, new_momentum = lax.optimization_barrier((rest, new_momentum))
        scale = float(max(experts * rows, cols)) ** 0.5
        update = exchange(orthogonal([own, *rest], scale).reshape(share.shape))
        whole = (experts, rows, cols)
        for j, part in enumerate([update, *others(update)]):
            whole = place(lax.rem(rep + j, n_rep), part, whole)
        return new_momentum, whole

    return jax.shard_map(
        shards,
        mesh=mesh,
        in_specs=(P(None, "shard", None), P(None, "shard", None)),
        out_specs=(P(None, "shard", None), P(None, "shard", None)),
        check_vma=False,
    )
```

```python
import functools

import jax
import jax.numpy as jnp
from jax import lax
from jax.experimental import pallas as pl
from jax.experimental.pallas import tpu as pltpu
from jax.sharding import PartitionSpec as P

ITERS = 5

coef_a = 3.4445
coef_b = -4.775
coef_c = 2.0315

LIMIT = 4.0

BF = jnp.bfloat16
F32 = jnp.float32


def next_momentum(m, g):
    return (0.95 * m.astype(F32) + g.astype(F32)).astype(BF)


def blend(m, g):
    return (g.astype(F32) + 0.95 * next_momentum(m, g).astype(F32)).astype(BF)


def share_kernel(rep_ref, m_hbm, g_hbm, share_hbm, m_ref, g_ref, share_ref, sems):
    experts, height, _ = share_ref.shape
    chunks = sems.shape[1]
    step = experts // chunks
    rows = pl.ds(pl.multiple_of(rep_ref[0] * height, height), height)
    copies = []
    for i in range(chunks):
        at = pl.ds(i * step, step)
        copies.append(
            [
                pltpu.make_async_copy(src.at[at, rows], dst.at[at], sems.at[j, i])
                for j, (src, dst) in enumerate(((m_hbm, m_ref), (g_hbm, g_ref)))
            ]
        )
        for copy in copies[-1]:
            copy.start()
    for i in range(chunks):
        for copy in copies[i]:
            copy.wait()
        at = slice(i * step, (i + 1) * step)
        share_ref[at] = blend(m_ref[at], g_ref[at])
        at = pl.ds(i * step, step)
        copies[i] = pltpu.make_async_copy(share_ref.at[at], share_hbm.at[at], sems.at[2, i])
        copies[i].start()
    for copy in copies:
        copy.wait()


def blended_share(rep, momentum, gradient, n_rep):
    experts, rows, cols = momentum.shape
    height = rows // n_rep
    shape = (experts, height, cols)
    if height % 16:
        m, g = (
            lax.dynamic_slice_in_dim(x, rep * height, height, 1) for x in (momentum, gradient)
        )
        return blend(m, g)
    chunks = 4 if experts % 4 == 0 else 1
    hbm = pl.BlockSpec(memory_space=pltpu.HBM)
    return pl.pallas_call(
        share_kernel,
        in_specs=[pl.BlockSpec(memory_space=pltpu.SMEM), hbm, hbm],
        out_specs=hbm,
        out_shape=jax.ShapeDtypeStruct(shape, BF),
        scratch_shapes=[
            pltpu.VMEM(shape, BF),
            pltpu.VMEM(shape, BF),
            pltpu.VMEM(shape, BF),
            pltpu.SemaphoreType.DMA((3, chunks)),
        ],
        compiler_params=pltpu.CompilerParams(vmem_limit_bytes=60 * 2**20),
        name="share",
    )(rep[None], momentum, gradient)


def momentum_kernel(m_ref, g_ref, new_ref):
    def one(e, carry):
        new_ref[e] = next_momentum(m_ref[e], g_ref[e])
        return carry

    lax.fori_loop(0, m_ref.shape[0], one, 0)


def new_momentum_of(momentum, gradient):
    vmem = pl.BlockSpec(memory_space=pltpu.VMEM)
    return pl.pallas_call(
        momentum_kernel,
        in_specs=[vmem, vmem],
        out_specs=vmem,
        out_shape=jax.ShapeDtypeStruct(momentum.shape, BF),
        cost_estimate=pl.CostEstimate(
            flops=2 * momentum.size, bytes_accessed=6 * momentum.size, transcendentals=0
        ),
        compiler_params=pltpu.CompilerParams(vmem_limit_bytes=16 * 2**20),
        name="new_momentum",
    )(momentum, gradient)


def halves(x):
    high = x.astype(BF)
    return high, (x - high.astype(F32)).astype(BF)


def dot(x, y):
    return jnp.dot(x, y, preferred_element_type=F32)


def dot_transposed(x, y, precision=None):
    return lax.dot_general(
        x, y, (((1,), (1,)), ((), ())), precision=precision, preferred_element_type=F32
    )


def orthogonal_kernel(scale, *refs):
    *parts, out_ref, x_ref, a_ref, s_ref, q_ref, left, right, full_ref = refs
    height, width = out_ref.shape
    n = x_ref.shape[0]
    half = n // 2
    for i, part in enumerate(parts):
        x_ref[i * height : (i + 1) * height] = part[...]

    def spread(blocks, to_left, to_right):
        b11, b12, b22 = blocks
        for i, j, x in ((0, 0, b11), (0, 1, b12), (1, 1, b22), (1, 0, b12.T)):
            high, low = halves(x)
            cols = slice(j * half, (j + 1) * half)
            if to_left:
                put_left(height + i * half, j * half, high, low)
            if to_right:
                for k, part in enumerate((high, low, high)):
                    right[k * n + i * half : k * n + (i + 1) * half, cols] = part

    def put_left(row, col, high, low):
        rows, cols = high.shape
        for k, part in enumerate((high, high, low)):
            left[row : row + rows, k * n + col : k * n + col + cols] = part

    def product(first=height):
        y = dot(left[first:], right[:, half:])
        z = dot(left[first : height + half], right[:, :half])
        q = height - first
        return (z[q:], y[q : q + half], y[q + half :]), z[:q], y[:q]

    def middle():
        a = [a_ref[i] for i in range(3)]
        spread(a, True, True)
        y, _, _ = product()
        m = [coef_b * u + coef_c * v for u, v in zip(a, y)]
        spread(m, False, True)
        return m

    def advance(y):
        for i in range(3):
            s_ref[i] = coef_a * a_ref[i] + y[i]
        spread([s_ref[i] for i in range(3)], True, False)
        y, _, _ = product()
        for i in range(3):
            a_ref[i] = coef_a * s_ref[i] + y[i]

    def extend():
        high, low = halves(q_ref[...])
        put_left(0, 0, high, low)

    y = dot_transposed(x_ref[...], x_ref[half:])
    gram = (dot_transposed(x_ref[:half], x_ref[:half]), y[:half], y[half:])
    eye = lax.broadcasted_iota(jnp.int32, (half, half), 0) == lax.broadcasted_iota(
        jnp.int32, (half, half), 1
    )
    square = jnp.sum(jnp.where(eye, gram[0] + gram[2], 0.0), keepdims=True)
    inverse = 1.0 / (jnp.sqrt(square) + 1e-07)
    for i in range(3):
        a_ref[i] = gram[i] * (inverse * inverse)

    m = middle()
    q_ref[:, :half] = (m[0] + jnp.where(eye, coef_a, 0.0))[:height]
    q_ref[:, half:] = m[1][:height]
    y, _, _ = product()
    advance(y)

    def step(_, carry):
        middle()
        extend()
        y, ql, qr = product(0)
        q_ref[:, :half] = coef_a * q_ref[:, :half] + ql
        q_ref[:, half:] = coef_a * q_ref[:, half:] + qr
        advance(y)
        return carry

    lax.fori_loop(1, ITERS - 1, step, 0)
    middle()
    extend()
    q = coef_a * q_ref[...] + dot(left[:height], right[...])
    spread_of_values = jnp.sum(q * q) * (1.0 / (height * n))
    good = spread_of_values < LIMIT

    @pl.when(good)
    def _():
        high, low = halves(q * (inverse * scale))
        left[:height, :n] = high
        left[:height, n : 2 * n] = low
        block = min(width, 512)
        for at in range(0, width, block):
            x = x_ref[:, at : at + block]
            out_ref[:, at : at + block] = (
                dot(left[:height, :n], x) + dot(left[:height, n : 2 * n], x)
            ).astype(BF)

    @pl.when(jnp.logical_not(good))
    def _():
        best = lax.Precision.HIGHEST
        block = min(width, 512)

        def columns(i):
            return pl.ds(pl.multiple_of(i * block, block), block)

        def load(i, carry):
            full_ref[:, columns(i)] = x_ref[:, columns(i)].astype(F32) * inverse
            return carry

        def sweep(_, carry):
            def add(i, total):
                x = full_ref[:, columns(i)]
                return total + dot_transposed(x, x, best)

            a = lax.fori_loop(0, width // block, add, jnp.zeros((n, n), F32))
            m = coef_b * a + coef_c * jnp.dot(a, a, precision=best)

            def apply(i, carry):
                x = full_ref[:, columns(i)]
                full_ref[:, columns(i)] = coef_a * x + jnp.dot(m, x, precision=best)
                return carry

            return lax.fori_loop(0, width // block, apply, carry)

        def store(i, carry):
            out_ref[:, columns(i)] = (full_ref[:height, columns(i)] * scale).astype(BF)
            return carry

        lax.fori_loop(0, width // block, load, 0)
        lax.fori_loop(0, ITERS, sweep, 0)
        lax.fori_loop(0, width // block, store, 0)


def orthogonal(parts, scale):
    height, cols = parts[0].shape
    n = height * len(parts)
    vmem = pl.BlockSpec(memory_space=pltpu.VMEM)
    return pl.pallas_call(
        functools.partial(orthogonal_kernel, scale),
        in_specs=[vmem] * len(parts),
        out_specs=vmem,
        out_shape=jax.ShapeDtypeStruct((height, cols), BF),
        scratch_shapes=[
            pltpu.VMEM((n, cols), BF),
            pltpu.VMEM((3, n // 2, n // 2), F32),
            pltpu.VMEM((3, n // 2, n // 2), F32),
            pltpu.VMEM((height, n), F32),
            pltpu.VMEM((height + n, 3 * n), BF),
            pltpu.VMEM((3 * n, n), BF),
            pltpu.VMEM((n, cols), F32),
        ],
        compiler_params=pltpu.CompilerParams(vmem_limit_bytes=40 * 2**20),
        name="orthogonal",
    )(*parts)


def place_kernel(rep_ref, part_ref, *refs):
    *_, out_ref, sems = refs
    experts, height, _ = part_ref.shape
    rows = pl.ds(pl.multiple_of(rep_ref[0] * height, height), height)
    step = experts // sems.shape[0]
    copies = []
    for i in range(sems.shape[0]):
        at = pl.ds(i * step, step)
        copies.append(pltpu.make_async_copy(part_ref.at[at], out_ref.at[at, rows], sems.at[i]))
        copies[-1].start()
    for copy in copies:
        copy.wait()


def place(which, part, whole):
    experts, height, cols = part.shape
    if height % 16:
        if isinstance(whole, tuple):
            whole = jnp.zeros(whole, BF)
        return lax.dynamic_update_slice(whole, part, (0, which * height, 0))
    anywhere = pl.BlockSpec(memory_space=pl.ANY)
    hbm = pl.BlockSpec(memory_space=pltpu.HBM)
    first = isinstance(whole, tuple)
    return pl.pallas_call(
        place_kernel,
        in_specs=[pl.BlockSpec(memory_space=pltpu.SMEM), anywhere] + [hbm] * (not first),
        out_specs=hbm,
        out_shape=jax.ShapeDtypeStruct(whole if first else whole.shape, BF),
        scratch_shapes=[pltpu.SemaphoreType.DMA((4 if experts % 4 == 0 else 1,))],
        input_output_aliases={} if first else {2: 0},
        cost_estimate=pl.CostEstimate(
            flops=0, bytes_accessed=4 * part.size, transcendentals=0
        ),
        compiler_params=pltpu.CompilerParams(vmem_limit_bytes=4 * 2**20),
        name="place",
    )(which[None], part, *([] if first else [whole]))


def solution(mesh):
    n_rep = mesh.shape["rep"]
    n_shard = mesh.shape["shard"]
    order = [p // 2 + p % 2 * (n_shard // 2) if n_shard % 2 == 0 else p for p in range(n_shard)]

    def others(x):
        return [
            lax.ppermute(x, "rep", [((i + j) % n_rep, i) for i in range(n_rep)])
            for j in range(1, n_rep)
        ]

    def exchange(x):
        return lax.all_to_all(
            x, "shard", split_axis=0, concat_axis=0, axis_index_groups=[order], tiled=True
        )

    def shards(momentum, gradient):
        experts, rows, cols = momentum.shape
        rep = lax.axis_index("rep")
        share = exchange(blended_share(rep, momentum, gradient, n_rep))
        own = share.reshape(-1, cols)
        rest = others(own)
        momentum, gradient, own = lax.optimization_barrier((momentum, gradient, own))
        new_momentum = new_momentum_of(momentum, gradient)
        rest, new_momentum = lax.optimization_barrier((rest, new_momentum))
        scale = float(max(experts * rows, cols)) ** 0.5
        update = exchange(orthogonal([own, *rest], scale).reshape(share.shape))
        whole = (experts, rows, cols)
        for j, part in enumerate([update, *others(update)]):
            whole = place(lax.rem(rep + j, n_rep), part, whole)
        return new_momentum, whole

    return jax.shard_map(
        shards,
        mesh=mesh,
        in_specs=(P(None, "shard", None), P(None, "shard", None)),
        out_specs=(P(None, "shard", None), P(None, "shard", None)),
        check_vma=False,
    )
```

```python
import functools

import jax
import jax.numpy as jnp
from jax import lax
from jax.experimental import pallas as pl
from jax.experimental.pallas import tpu as pltpu
from jax.sharding import PartitionSpec as P

ITERS = 5

coef_a = 3.4445
coef_b = -4.775
coef_c = 2.0315

LIMIT = 4.0

BF = jnp.bfloat16
F32 = jnp.float32


def next_momentum(m, g):
    return (0.95 * m.astype(F32) + g.astype(F32)).astype(BF)


def blend(m, g):
    return (g.astype(F32) + 0.95 * next_momentum(m, g).astype(F32)).astype(BF)


def share_kernel(rep_ref, m_hbm, g_hbm, share_hbm, m_ref, g_ref, share_ref, sems):
    experts, height, _ = share_ref.shape
    chunks = sems.shape[1]
    step = experts // chunks
    rows = pl.ds(pl.multiple_of(rep_ref[0] * height, height), height)
    copies = []
    for i in range(chunks):
        at = pl.ds(i * step, step)
        copies.append(
            [
                pltpu.make_async_copy(src.at[at, rows], dst.at[at], sems.at[j, i])
                for j, (src, dst) in enumerate(((m_hbm, m_ref), (g_hbm, g_ref)))
            ]
        )
        for copy in copies[-1]:
            copy.start()
    for i in range(chunks):
        for copy in copies[i]:
            copy.wait()
        at = slice(i * step, (i + 1) * step)
        share_ref[at] = blend(m_ref[at], g_ref[at])
        at = pl.ds(i * step, step)
        copies[i] = pltpu.make_async_copy(share_ref.at[at], share_hbm.at[at], sems.at[2, i])
        copies[i].start()
    for copy in copies:
        copy.wait()


def blended_share(rep, momentum, gradient, n_rep):
    experts, rows, cols = momentum.shape
    height = rows // n_rep
    shape = (experts, height, cols)
    if height % 16:
        m, g = (
            lax.dynamic_slice_in_dim(x, rep * height, height, 1) for x in (momentum, gradient)
        )
        return blend(m, g)
    chunks = 4 if experts % 4 == 0 else 1
    hbm = pl.BlockSpec(memory_space=pltpu.HBM)
    return pl.pallas_call(
        share_kernel,
        in_specs=[pl.BlockSpec(memory_space=pltpu.SMEM), hbm, hbm],
        out_specs=hbm,
        out_shape=jax.ShapeDtypeStruct(shape, BF),
        scratch_shapes=[
            pltpu.VMEM(shape, BF),
            pltpu.VMEM(shape, BF),
            pltpu.VMEM(shape, BF),
            pltpu.SemaphoreType.DMA((3, chunks)),
        ],
        compiler_params=pltpu.CompilerParams(vmem_limit_bytes=60 * 2**20),
        name="share",
    )(rep[None], momentum, gradient)


def momentum_kernel(m_ref, g_ref, new_ref):
    def one(e, carry):
        new_ref[e] = next_momentum(m_ref[e], g_ref[e])
        return carry

    lax.fori_loop(0, m_ref.shape[0], one, 0)


def new_momentum_of(momentum, gradient):
    vmem = pl.BlockSpec(memory_space=pltpu.VMEM)
    return pl.pallas_call(
        momentum_kernel,
        in_specs=[vmem, vmem],
        out_specs=vmem,
        out_shape=jax.ShapeDtypeStruct(momentum.shape, BF),
        cost_estimate=pl.CostEstimate(
            flops=2 * momentum.size, bytes_accessed=6 * momentum.size, transcendentals=0
        ),
        compiler_params=pltpu.CompilerParams(vmem_limit_bytes=16 * 2**20),
        name="new_momentum",
    )(momentum, gradient)


def halves(x):
    high = x.astype(BF)
    return high, (x - high.astype(F32)).astype(BF)


def dot(x, y):
    return jnp.dot(x, y, preferred_element_type=F32)


def dot_transposed(x, y, precision=None):
    return lax.dot_general(
        x, y, (((1,), (1,)), ((), ())), precision=precision, preferred_element_type=F32
    )


def orthogonal_kernel(scale, *refs):
    *parts, out_ref, x_ref, a_ref, s_ref, q_ref, left, right, full_ref = refs
    height, width = out_ref.shape
    n = x_ref.shape[0]
    half = n // 2
    for i, part in enumerate(parts):
        x_ref[i * height : (i + 1) * height] = part[...]

    def spread(blocks, to_left, to_right):
        b11, b12, b22 = blocks
        for i, j, x in ((0, 0, b11), (0, 1, b12), (1, 1, b22), (1, 0, b12.T)):
            high, low = halves(x)
            cols = slice(j * half, (j + 1) * half)
            if to_left:
                put_left(height + i * half, j * half, high, low)
            if to_right:
                for k, part in enumerate((high, low, high)):
                    right[k * n + i * half : k * n + (i + 1) * half, cols] = part

    def put_left(row, col, high, low):
        rows, cols = high.shape
        for k, part in enumerate((high, high, low)):
            left[row : row + rows, k * n + col : k * n + col + cols] = part

    def product():
        upper = dot(left[height : height + half], right[...])
        corner = dot(left[height + half :], right[:, half:])
        return upper[:, :half], upper[:, half:], corner

    def middle():
        a = [a_ref[i] for i in range(3)]
        spread(a, True, True)
        y = product()
        m = [coef_b * u + coef_c * v for u, v in zip(a, y)]
        spread(m, False, True)
        return m

    def advance():
        s = [coef_a * a_ref[i] + y for i, y in enumerate(product())]
        for i in range(3):
            s_ref[i] = s[i]
        spread(s, True, False)
        y = product()
        for i in range(3):
            a_ref[i] = coef_a * s_ref[i] + y[i]

    def rows_times(q):
        high, low = halves(q)
        put_left(0, 0, high, low)
        return dot(left[:height], right[...])

    y = dot_transposed(x_ref[...], x_ref[half:])
    gram = (dot_transposed(x_ref[:half], x_ref[:half]), y[:half], y[half:])
    eye = lax.broadcasted_iota(jnp.int32, (half, half), 0) == lax.broadcasted_iota(
        jnp.int32, (half, half), 1
    )
    square = jnp.sum(jnp.where(eye, gram[0] + gram[2], 0.0), keepdims=True)
    inverse = 1.0 / (jnp.sqrt(square) + 1e-07)
    for i in range(3):
        a_ref[i] = gram[i] * (inverse * inverse)

    m = middle()
    q_ref[:, :half] = (m[0] + jnp.where(eye, coef_a, 0.0))[:height]
    q_ref[:, half:] = m[1][:height]
    advance()

    def step(_, carry):
        middle()
        advance()
        q_ref[...] = coef_a * q_ref[...] + rows_times(q_ref[...])
        return carry

    lax.fori_loop(1, ITERS - 1, step, 0)
    spread([a_ref[i] for i in range(3)], False, True)
    q = q_ref[...]
    q = coef_a * q + rows_times(coef_b * q + coef_c * rows_times(q))
    spread_of_values = jnp.sum(q * q) * (1.0 / (height * n))
    good = spread_of_values < LIMIT

    @pl.when(good)
    def _():
        high, low = halves(q * (inverse * scale))
        left[:height, :n] = high
        left[:height, n : 2 * n] = low
        block = min(width, 512)
        for at in range(0, width, block):
            x = x_ref[:, at : at + block]
            out_ref[:, at : at + block] = (
                dot(left[:height, :n], x) + dot(left[:height, n : 2 * n], x)
            ).astype(BF)

    @pl.when(jnp.logical_not(good))
    def _():
        best = lax.Precision.HIGHEST
        block = min(width, 512)

        def columns(i):
            return pl.ds(pl.multiple_of(i * block, block), block)

        def load(i, carry):
            full_ref[:, columns(i)] = x_ref[:, columns(i)].astype(F32) * inverse
            return carry

        def sweep(_, carry):
            def add(i, total):
                x = full_ref[:, columns(i)]
                return total + dot_transposed(x, x, best)

            a = lax.fori_loop(0, width // block, add, jnp.zeros((n, n), F32))
            m = coef_b * a + coef_c * jnp.dot(a, a, precision=best)

            def apply(i, carry):
                x = full_ref[:, columns(i)]
                full_ref[:, columns(i)] = coef_a * x + jnp.dot(m, x, precision=best)
                return carry

            return lax.fori_loop(0, width // block, apply, carry)

        def store(i, carry):
            out_ref[:, columns(i)] = (full_ref[:height, columns(i)] * scale).astype(BF)
            return carry

        lax.fori_loop(0, width // block, load, 0)
        lax.fori_loop(0, ITERS, sweep, 0)
        lax.fori_loop(0, width // block, store, 0)


def orthogonal(parts, scale):
    height, cols = parts[0].shape
    n = height * len(parts)
    vmem = pl.BlockSpec(memory_space=pltpu.VMEM)
    return pl.pallas_call(
        functools.partial(orthogonal_kernel, scale),
        in_specs=[vmem] * len(parts),
        out_specs=vmem,
        out_shape=jax.ShapeDtypeStruct((height, cols), BF),
        scratch_shapes=[
            pltpu.VMEM((n, cols), BF),
            pltpu.VMEM((3, n // 2, n // 2), F32),
            pltpu.VMEM((3, n // 2, n // 2), F32),
            pltpu.VMEM((height, n), F32),
            pltpu.VMEM((height + n, 3 * n), BF),
            pltpu.VMEM((3 * n, n), BF),
            pltpu.VMEM((n, cols), F32),
        ],
        compiler_params=pltpu.CompilerParams(vmem_limit_bytes=40 * 2**20),
        name="orthogonal",
    )(*parts)


def place_kernel(rep_ref, part_ref, *refs):
    *_, out_ref, sems = refs
    experts, height, _ = part_ref.shape
    rows = pl.ds(pl.multiple_of(rep_ref[0] * height, height), height)
    step = experts // sems.shape[0]
    copies = []
    for i in range(sems.shape[0]):
        at = pl.ds(i * step, step)
        copies.append(pltpu.make_async_copy(part_ref.at[at], out_ref.at[at, rows], sems.at[i]))
        copies[-1].start()
    for copy in copies:
        copy.wait()


def place(which, part, whole):
    experts, height, cols = part.shape
    if height % 16:
        if isinstance(whole, tuple):
            whole = jnp.zeros(whole, BF)
        return lax.dynamic_update_slice(whole, part, (0, which * height, 0))
    anywhere = pl.BlockSpec(memory_space=pl.ANY)
    hbm = pl.BlockSpec(memory_space=pltpu.HBM)
    first = isinstance(whole, tuple)
    return pl.pallas_call(
        place_kernel,
        in_specs=[pl.BlockSpec(memory_space=pltpu.SMEM), anywhere] + [hbm] * (not first),
        out_specs=hbm,
        out_shape=jax.ShapeDtypeStruct(whole if first else whole.shape, BF),
        scratch_shapes=[pltpu.SemaphoreType.DMA((4 if experts % 4 == 0 else 1,))],
        input_output_aliases={} if first else {2: 0},
        cost_estimate=pl.CostEstimate(
            flops=0, bytes_accessed=4 * part.size, transcendentals=0
        ),
        compiler_params=pltpu.CompilerParams(vmem_limit_bytes=4 * 2**20),
        name="place",
    )(which[None], part, *([] if first else [whole]))


def solution(mesh):
    n_rep = mesh.shape["rep"]
    n_shard = mesh.shape["shard"]
    order = [p // 2 + p % 2 * (n_shard // 2) if n_shard % 2 == 0 else p for p in range(n_shard)]

    def others(x):
        return [
            lax.ppermute(x, "rep", [((i + j) % n_rep, i) for i in range(n_rep)])
            for j in range(1, n_rep)
        ]

    def exchange(x):
        return lax.all_to_all(
            x, "shard", split_axis=0, concat_axis=0, axis_index_groups=[order], tiled=True
        )

    def shards(momentum, gradient):
        experts, rows, cols = momentum.shape
        rep = lax.axis_index("rep")
        share = exchange(blended_share(rep, momentum, gradient, n_rep))
        own = share.reshape(-1, cols)
        rest = others(own)
        momentum, gradient, own = lax.optimization_barrier((momentum, gradient, own))
        new_momentum = new_momentum_of(momentum, gradient)
        rest, new_momentum = lax.optimization_barrier((rest, new_momentum))
        scale = float(max(experts * rows, cols)) ** 0.5
        update = exchange(orthogonal([own, *rest], scale).reshape(share.shape))
        whole = (experts, rows, cols)
        for j, part in enumerate([update, *others(update)]):
            whole = place(lax.rem(rep + j, n_rep), part, whole)
        return new_momentum, whole

    return jax.shard_map(
        shards,
        mesh=mesh,
        in_specs=(P(None, "shard", None), P(None, "shard", None)),
        out_specs=(P(None, "shard", None), P(None, "shard", None)),
        check_vma=False,
    )
```

```python
import functools

import jax
import jax.numpy as jnp
from jax import lax
from jax.experimental import pallas as pl
from jax.experimental.pallas import tpu as pltpu
from jax.sharding import PartitionSpec as P

ITERS = 5

coef_a = 3.4445
coef_b = -4.775
coef_c = 2.0315

LIMIT = 4.0

BF = jnp.bfloat16
F32 = jnp.float32


def next_momentum(m, g):
    return (0.95 * m.astype(F32) + g.astype(F32)).astype(BF)


def blend(m, g):
    return (g.astype(F32) + 0.95 * next_momentum(m, g).astype(F32)).astype(BF)


def share_kernel(rep_ref, m_hbm, g_hbm, share_hbm, m_ref, g_ref, share_ref, sems):
    experts, height, _ = share_ref.shape
    chunks = sems.shape[1]
    step = experts // chunks
    rows = pl.ds(pl.multiple_of(rep_ref[0] * height, height), height)
    copies = []
    for i in range(chunks):
        at = pl.ds(i * step, step)
        copies.append(
            [
                pltpu.make_async_copy(src.at[at, rows], dst.at[at], sems.at[j, i])
                for j, (src, dst) in enumerate(((m_hbm, m_ref), (g_hbm, g_ref)))
            ]
        )
        for copy in copies[-1]:
            copy.start()
    for i in range(chunks):
        for copy in copies[i]:
            copy.wait()
        at = slice(i * step, (i + 1) * step)
        share_ref[at] = blend(m_ref[at], g_ref[at])
        at = pl.ds(i * step, step)
        copies[i] = pltpu.make_async_copy(share_ref.at[at], share_hbm.at[at], sems.at[2, i])
        copies[i].start()
    for copy in copies:
        copy.wait()


def blended_share(rep, momentum, gradient, n_rep):
    experts, rows, cols = momentum.shape
    height = rows // n_rep
    shape = (experts, height, cols)
    if height % 16:
        m, g = (
            lax.dynamic_slice_in_dim(x, rep * height, height, 1) for x in (momentum, gradient)
        )
        return blend(m, g)
    chunks = 4 if experts % 4 == 0 else 1
    hbm = pl.BlockSpec(memory_space=pltpu.HBM)
    return pl.pallas_call(
        share_kernel,
        in_specs=[pl.BlockSpec(memory_space=pltpu.SMEM), hbm, hbm],
        out_specs=hbm,
        out_shape=jax.ShapeDtypeStruct(shape, BF),
        scratch_shapes=[
            pltpu.VMEM(shape, BF),
            pltpu.VMEM(shape, BF),
            pltpu.VMEM(shape, BF),
            pltpu.SemaphoreType.DMA((3, chunks)),
        ],
        compiler_params=pltpu.CompilerParams(vmem_limit_bytes=60 * 2**20),
        name="share",
    )(rep[None], momentum, gradient)


def momentum_kernel(m_ref, g_ref, new_ref):
    def one(e, carry):
        new_ref[e] = next_momentum(m_ref[e], g_ref[e])
        return carry

    lax.fori_loop(0, m_ref.shape[0], one, 0)


def new_momentum_of(momentum, gradient):
    vmem = pl.BlockSpec(memory_space=pltpu.VMEM)
    return pl.pallas_call(
        momentum_kernel,
        in_specs=[vmem, vmem],
        out_specs=vmem,
        out_shape=jax.ShapeDtypeStruct(momentum.shape, BF),
        cost_estimate=pl.CostEstimate(
            flops=2 * momentum.size, bytes_accessed=6 * momentum.size, transcendentals=0
        ),
        compiler_params=pltpu.CompilerParams(vmem_limit_bytes=16 * 2**20),
        name="new_momentum",
    )(momentum, gradient)


def halves(x):
    high = x.astype(BF)
    return high, (x - high.astype(F32)).astype(BF)


def dot(x, y):
    return jnp.dot(x, y, preferred_element_type=F32)


def dot_transposed(x, y, precision=None):
    return lax.dot_general(
        x, y, (((1,), (1,)), ((), ())), precision=precision, preferred_element_type=F32
    )


def orthogonal_kernel(scale, *refs):
    *parts, out_ref, x_ref, a_ref, s_ref, q_ref = refs[:-6]
    a_left, a_right, m_right, s_left, q_left, full_ref = refs[-6:]
    height, width = out_ref.shape
    n = x_ref.shape[0]
    half = n // 2
    for i, part in enumerate(parts):
        x_ref[i * height : (i + 1) * height] = part[...]

    blocks = ((0, 1), (0, 0), (1, 1))

    def rows(i):
        return slice(i * half, (i + 1) * half)

    def put_left(ref, row, col, high, low):
        height, width = high.shape
        for k, part in enumerate((high, high, low)):
            ref[row : row + height, k * n + col : k * n + col + width] = part

    def put(i, j, x, left=None, right=None):
        for i, j, x in ((i, j, x), (j, i, x.T))[: 1 + (i != j)]:
            high, low = halves(x)
            if left is not None:
                put_left(left, i * half, j * half, high, low)
            if right is not None:
                for k, part in enumerate((high, low, high)):
                    right[k * n + i * half : k * n + (i + 1) * half, rows(j)] = part

    def put_q(q):
        q_ref[...] = q
        high, low = halves(q)
        put_left(q_left, 0, 0, high, low)

    def put_a(i, j, a):
        a_ref[i + j] = a
        put(i, j, a, a_left, a_right)

    eye = lax.broadcasted_iota(jnp.int32, (half, half), 0) == lax.broadcasted_iota(
        jnp.int32, (half, half), 1
    )
    gram = {(i, j): dot_transposed(x_ref[rows(i)], x_ref[rows(j)]) for i, j in blocks}
    square = jnp.sum(jnp.where(eye, gram[0, 0] + gram[1, 1], 0.0), keepdims=True)
    inverse = 1.0 / (jnp.sqrt(square) + 1e-07)
    for i, j in blocks:
        put_a(i, j, gram[i, j] * (inverse * inverse))

    for sweep in range(ITERS - 1):
        for i, j in blocks:
            m = coef_b * a_ref[i + j] + coef_c * dot(a_left[rows(i)], a_right[:, rows(j)])
            put(i, j, m, right=m_right)
            if sweep == 0 and i == 0:
                p = m + jnp.where(eye, coef_a, 0.0) if j == 0 else m
                q_ref[:, rows(j)] = p[:height]
        for i, j in blocks:
            s = coef_a * a_ref[i + j] + dot(a_left[rows(i)], m_right[:, rows(j)])
            s_ref[i + j] = s
            put(i, j, s, left=s_left)
        q = q_ref[...]
        put_q(coef_a * q + dot(q_left[...], m_right[...]) if sweep else q)
        for i, j in blocks:
            put_a(i, j, coef_a * s_ref[i + j] + dot(s_left[rows(i)], m_right[:, rows(j)]))

    q = q_ref[...]
    high, low = halves(coef_b * q + coef_c * dot(q_left[...], a_right[...]))
    put_left(s_left, 0, 0, high, low)
    q = coef_a * q + dot(s_left[:height], a_right[...])
    spread_of_values = jnp.sum(q * q) * (1.0 / (height * n))
    good = spread_of_values < LIMIT

    @pl.when(good)
    def _():
        high, low = halves(q * (inverse * scale))
        q_left[:, :n] = high
        q_left[:, n : 2 * n] = low
        block = min(width, 512)
        for at in range(0, width, block):
            x = x_ref[:, at : at + block]
            out_ref[:, at : at + block] = (
                dot(q_left[:, :n], x) + dot(q_left[:, n : 2 * n], x)
            ).astype(BF)

    @pl.when(jnp.logical_not(good))
    def _():
        best = lax.Precision.HIGHEST
        block = min(width, 512)

        def columns(i):
            return pl.ds(pl.multiple_of(i * block, block), block)

        def load(i, carry):
            full_ref[:, columns(i)] = x_ref[:, columns(i)].astype(F32) * inverse
            return carry

        def sweep(_, carry):
            def add(i, total):
                x = full_ref[:, columns(i)]
                return total + dot_transposed(x, x, best)

            a = lax.fori_loop(0, width // block, add, jnp.zeros((n, n), F32))
            m = coef_b * a + coef_c * jnp.dot(a, a, precision=best)

            def apply(i, carry):
                x = full_ref[:, columns(i)]
                full_ref[:, columns(i)] = coef_a * x + jnp.dot(m, x, precision=best)
                return carry

            return lax.fori_loop(0, width // block, apply, carry)

        def store(i, carry):
            out_ref[:, columns(i)] = (full_ref[:height, columns(i)] * scale).astype(BF)
            return carry

        lax.fori_loop(0, width // block, load, 0)
        lax.fori_loop(0, ITERS, sweep, 0)
        lax.fori_loop(0, width // block, store, 0)


def orthogonal(parts, scale):
    height, cols = parts[0].shape
    n = height * len(parts)
    vmem = pl.BlockSpec(memory_space=pltpu.VMEM)
    return pl.pallas_call(
        functools.partial(orthogonal_kernel, scale),
        in_specs=[vmem] * len(parts),
        out_specs=vmem,
        out_shape=jax.ShapeDtypeStruct((height, cols), BF),
        scratch_shapes=[
            pltpu.VMEM((n, cols), BF),
            pltpu.VMEM((3, n // 2, n // 2), F32),
            pltpu.VMEM((3, n // 2, n // 2), F32),
            pltpu.VMEM((height, n), F32),
            pltpu.VMEM((n, 3 * n), BF),
            pltpu.VMEM((3 * n, n), BF),
            pltpu.VMEM((3 * n, n), BF),
            pltpu.VMEM((n, 3 * n), BF),
            pltpu.VMEM((height, 3 * n), BF),
            pltpu.VMEM((n, cols), F32),
        ],
        compiler_params=pltpu.CompilerParams(vmem_limit_bytes=40 * 2**20),
        name="orthogonal",
    )(*parts)


def place_kernel(rep_ref, part_ref, *refs):
    *_, out_ref, sems = refs
    experts, height, _ = part_ref.shape
    rows = pl.ds(pl.multiple_of(rep_ref[0] * height, height), height)
    step = experts // sems.shape[0]
    copies = []
    for i in range(sems.shape[0]):
        at = pl.ds(i * step, step)
        copies.append(pltpu.make_async_copy(part_ref.at[at], out_ref.at[at, rows], sems.at[i]))
        copies[-1].start()
    for copy in copies:
        copy.wait()


def place(which, part, whole):
    experts, height, cols = part.shape
    if height % 16:
        if isinstance(whole, tuple):
            whole = jnp.zeros(whole, BF)
        return lax.dynamic_update_slice(whole, part, (0, which * height, 0))
    anywhere = pl.BlockSpec(memory_space=pl.ANY)
    hbm = pl.BlockSpec(memory_space=pltpu.HBM)
    first = isinstance(whole, tuple)
    return pl.pallas_call(
        place_kernel,
        in_specs=[pl.BlockSpec(memory_space=pltpu.SMEM), anywhere] + [hbm] * (not first),
        out_specs=hbm,
        out_shape=jax.ShapeDtypeStruct(whole if first else whole.shape, BF),
        scratch_shapes=[pltpu.SemaphoreType.DMA((4 if experts % 4 == 0 else 1,))],
        input_output_aliases={} if first else {2: 0},
        cost_estimate=pl.CostEstimate(
            flops=0, bytes_accessed=4 * part.size, transcendentals=0
        ),
        compiler_params=pltpu.CompilerParams(vmem_limit_bytes=4 * 2**20),
        name="place",
    )(which[None], part, *([] if first else [whole]))


def solution(mesh):
    n_rep = mesh.shape["rep"]

    def others(x):
        return [
            lax.ppermute(x, "rep", [((i + j) % n_rep, i) for i in range(n_rep)])
            for j in range(1, n_rep)
        ]

    def exchange(x):
        return lax.all_to_all(x, "shard", split_axis=0, concat_axis=0, tiled=True)

    def shards(momentum, gradient):
        experts, rows, cols = momentum.shape
        rep = lax.axis_index("rep")
        share = exchange(blended_share(rep, momentum, gradient, n_rep))
        own = share.reshape(-1, cols)
        rest = others(own)
        momentum, gradient, own = lax.optimization_barrier((momentum, gradient, own))
        new_momentum = new_momentum_of(momentum, gradient)
        rest, new_momentum = lax.optimization_barrier((rest, new_momentum))
        scale = float(max(experts * rows, cols)) ** 0.5
        update = exchange(orthogonal([own, *rest], scale).reshape(share.shape))
        whole = (experts, rows, cols)
        for j, part in enumerate([update, *others(update)]):
            whole = place(lax.rem(rep + j, n_rep), part, whole)
        return new_momentum, whole

    return jax.shard_map(
        shards,
        mesh=mesh,
        in_specs=(P(None, "shard", None), P(None, "shard", None)),
        out_specs=(P(None, "shard", None), P(None, "shard", None)),
        check_vma=False,
    )
```

```python
import functools

import jax
import jax.numpy as jnp
from jax import lax
from jax.experimental import pallas as pl
from jax.experimental.pallas import tpu as pltpu
from jax.sharding import PartitionSpec as P

ITERS = 5

coef_a = 3.4445
coef_b = -4.775
coef_c = 2.0315

LIMIT = 4.0

BF = jnp.bfloat16
F32 = jnp.float32


def next_momentum(m, g):
    return (0.95 * m.astype(F32) + g.astype(F32)).astype(BF)


def blend(m, g):
    return (g.astype(F32) + 0.95 * next_momentum(m, g).astype(F32)).astype(BF)


def share_kernel(at_ref, m_hbm, g_hbm, *refs):
    *share_hbms, m_ref, g_ref, share_ref, sems = refs
    count = len(share_hbms)
    experts = m_hbm.shape[0]
    copies = []
    for j in range(count):
        e = lax.rem(at_ref[0] + j * (experts // count), experts)
        copies.append(
            [
                pltpu.make_async_copy(src.at[e], dst.at[j], sems.at[i, j])
                for i, (src, dst) in enumerate(((m_hbm, m_ref), (g_hbm, g_ref)))
            ]
        )
        for copy in copies[-1]:
            copy.start()
    for j, share_hbm in enumerate(share_hbms):
        for copy in copies[j]:
            copy.wait()
        share_ref[j] = blend(m_ref[j], g_ref[j])
        copies[j] = pltpu.make_async_copy(share_ref.at[j], share_hbm, sems.at[2, j])
        copies[j].start()
    for copy in copies:
        copy.wait()


def blended_share(first, momentum, gradient, count):
    experts, rows, cols = momentum.shape
    hbm = pl.BlockSpec(memory_space=pltpu.HBM)
    return pl.pallas_call(
        share_kernel,
        in_specs=[pl.BlockSpec(memory_space=pltpu.SMEM), hbm, hbm],
        out_specs=[hbm] * count,
        out_shape=[jax.ShapeDtypeStruct((rows, cols), BF)] * count,
        scratch_shapes=[pltpu.VMEM((count, rows, cols), BF)] * 3
        + [pltpu.SemaphoreType.DMA((3, count))],
        compiler_params=pltpu.CompilerParams(vmem_limit_bytes=60 * 2**20),
        name="share",
    )(first[None], momentum, gradient)


def momentum_kernel(m_ref, g_ref, new_ref):
    def one(e, carry):
        new_ref[e] = next_momentum(m_ref[e], g_ref[e])
        return carry

    lax.fori_loop(0, m_ref.shape[0], one, 0)


def new_momentum_of(momentum, gradient):
    vmem = pl.BlockSpec(memory_space=pltpu.VMEM)
    return pl.pallas_call(
        momentum_kernel,
        in_specs=[vmem, vmem],
        out_specs=vmem,
        out_shape=jax.ShapeDtypeStruct(momentum.shape, BF),
        cost_estimate=pl.CostEstimate(
            flops=2 * momentum.size, bytes_accessed=6 * momentum.size, transcendentals=0
        ),
        compiler_params=pltpu.CompilerParams(vmem_limit_bytes=16 * 2**20),
        name="new_momentum",
    )(momentum, gradient)


def halves(x):
    high = x.astype(BF)
    return high, (x - high.astype(F32)).astype(BF)


def dot(x, y):
    return jnp.dot(x, y, preferred_element_type=F32)


def dot_transposed(x, y, precision=None):
    return lax.dot_general(
        x, y, (((1,), (1,)), ((), ())), precision=precision, preferred_element_type=F32
    )


def orthogonal_kernel(scale, count, *refs):
    *parts, x_ref, a_ref, s_ref, q_ref = refs[:-6]
    parts, out_refs = parts[:-count], parts[-count:]
    a_left, a_right, m_right, s_left, q_left, full_ref = refs[-6:]
    piece, width = out_refs[0].shape
    height = count * piece
    n = x_ref.shape[0]
    half = n // 2
    for i, part in enumerate(parts):
        x_ref[i * piece : (i + 1) * piece] = part[...]

    def put_out(cols, y):
        for i, out_ref in enumerate(out_refs):
            out_ref[:, cols] = y[i * piece : (i + 1) * piece].astype(BF)

    blocks = ((0, 1), (0, 0), (1, 1))

    def rows(i):
        return slice(i * half, (i + 1) * half)

    def put_left(ref, row, col, high, low):
        height, width = high.shape
        for k, part in enumerate((high, high, low)):
            ref[row : row + height, k * n + col : k * n + col + width] = part

    def put(i, j, x, left=None, right=None):
        for i, j, x in ((i, j, x), (j, i, x.T))[: 1 + (i != j)]:
            high, low = halves(x)
            if left is not None:
                put_left(left, i * half, j * half, high, low)
            if right is not None:
                for k, part in enumerate((high, low, high)):
                    right[k * n + i * half : k * n + (i + 1) * half, rows(j)] = part

    def put_q(q):
        q_ref[...] = q
        high, low = halves(q)
        put_left(q_left, 0, 0, high, low)

    def put_a(i, j, a):
        a_ref[i + j] = a
        put(i, j, a, a_left, a_right)

    eye = lax.broadcasted_iota(jnp.int32, (half, half), 0) == lax.broadcasted_iota(
        jnp.int32, (half, half), 1
    )
    gram = {(i, j): dot_transposed(x_ref[rows(i)], x_ref[rows(j)]) for i, j in blocks}
    square = jnp.sum(jnp.where(eye, gram[0, 0] + gram[1, 1], 0.0), keepdims=True)
    inverse = 1.0 / (jnp.sqrt(square) + 1e-07)
    for i, j in blocks:
        put_a(i, j, gram[i, j] * (inverse * inverse))

    for sweep in range(ITERS - 1):
        for i, j in blocks:
            m = coef_b * a_ref[i + j] + coef_c * dot(a_left[rows(i)], a_right[:, rows(j)])
            put(i, j, m, right=m_right)
            if sweep == 0 and i == 0:
                p = m + jnp.where(eye, coef_a, 0.0) if j == 0 else m
                q_ref[:, rows(j)] = p[:height]
        for i, j in blocks:
            s = coef_a * a_ref[i + j] + dot(a_left[rows(i)], m_right[:, rows(j)])
            s_ref[i + j] = s
            put(i, j, s, left=s_left)
        q = q_ref[...]
        put_q(coef_a * q + dot(q_left[...], m_right[...]) if sweep else q)
        for i, j in blocks:
            put_a(i, j, coef_a * s_ref[i + j] + dot(s_left[rows(i)], m_right[:, rows(j)]))

    q = q_ref[...]
    high, low = halves(coef_b * q + coef_c * dot(q_left[...], a_right[...]))
    put_left(s_left, 0, 0, high, low)
    q = coef_a * q + dot(s_left[:height], a_right[...])
    spread_of_values = jnp.sum(q * q) * (1.0 / (height * n))
    good = spread_of_values < LIMIT

    @pl.when(good)
    def _():
        high, low = halves(q * (inverse * scale))
        q_left[:, :n] = high
        q_left[:, n : 2 * n] = low
        block = min(width, 512)
        for at in range(0, width, block):
            x = x_ref[:, at : at + block]
            y = dot(q_left[:, :n], x) + dot(q_left[:, n : 2 * n], x)
            put_out(slice(at, at + block), y)

    @pl.when(jnp.logical_not(good))
    def _():
        best = lax.Precision.HIGHEST
        block = min(width, 512)

        def columns(i):
            return pl.ds(pl.multiple_of(i * block, block), block)

        def load(i, carry):
            full_ref[:, columns(i)] = x_ref[:, columns(i)].astype(F32) * inverse
            return carry

        def sweep(_, carry):
            def add(i, total):
                x = full_ref[:, columns(i)]
                return total + dot_transposed(x, x, best)

            a = lax.fori_loop(0, width // block, add, jnp.zeros((n, n), F32))
            m = coef_b * a + coef_c * jnp.dot(a, a, precision=best)

            def apply(i, carry):
                x = full_ref[:, columns(i)]
                full_ref[:, columns(i)] = coef_a * x + jnp.dot(m, x, precision=best)
                return carry

            return lax.fori_loop(0, width // block, apply, carry)

        def store(i, carry):
            put_out(columns(i), full_ref[:height, columns(i)] * scale)
            return carry

        lax.fori_loop(0, width // block, load, 0)
        lax.fori_loop(0, ITERS, sweep, 0)
        lax.fori_loop(0, width // block, store, 0)


def orthogonal(parts, count, scale):
    piece, cols = parts[0].shape
    height = piece * count
    n = piece * len(parts)
    vmem = pl.BlockSpec(memory_space=pltpu.VMEM)
    return pl.pallas_call(
        functools.partial(orthogonal_kernel, scale, count),
        in_specs=[vmem] * len(parts),
        out_specs=[vmem] * count,
        out_shape=[jax.ShapeDtypeStruct((piece, cols), BF)] * count,
        scratch_shapes=[
            pltpu.VMEM((n, cols), BF),
            pltpu.VMEM((3, n // 2, n // 2), F32),
            pltpu.VMEM((3, n // 2, n // 2), F32),
            pltpu.VMEM((height, n), F32),
            pltpu.VMEM((n, 3 * n), BF),
            pltpu.VMEM((3 * n, n), BF),
            pltpu.VMEM((3 * n, n), BF),
            pltpu.VMEM((n, 3 * n), BF),
            pltpu.VMEM((height, 3 * n), BF),
            pltpu.VMEM((n, cols), F32),
        ],
        compiler_params=pltpu.CompilerParams(vmem_limit_bytes=40 * 2**20),
        name="orthogonal",
    )(*parts)


def place_kernel(count, at_ref, *refs):
    parts, (*_, out_ref, sems) = refs[:count], refs[count:]
    experts = out_ref.shape[0]
    copies = []
    for j, part in enumerate(parts):
        e = lax.rem(at_ref[0] + j * (experts // count), experts)
        copies.append(pltpu.make_async_copy(part, out_ref.at[e], sems.at[j]))
        copies[-1].start()
    for copy in copies:
        copy.wait()


def place(first, parts, whole):
    count = len(parts)
    anywhere = pl.BlockSpec(memory_space=pl.ANY)
    hbm = pl.BlockSpec(memory_space=pltpu.HBM)
    new = isinstance(whole, tuple)
    return pl.pallas_call(
        functools.partial(place_kernel, count),
        in_specs=[pl.BlockSpec(memory_space=pltpu.SMEM)] + [anywhere] * count + [hbm] * (not new),
        out_specs=hbm,
        out_shape=jax.ShapeDtypeStruct(whole if new else whole.shape, BF),
        scratch_shapes=[pltpu.SemaphoreType.DMA((count,))],
        input_output_aliases={} if new else {count + 1: 0},
        cost_estimate=pl.CostEstimate(
            flops=0, bytes_accessed=4 * count * parts[0].size, transcendentals=0
        ),
        compiler_params=pltpu.CompilerParams(vmem_limit_bytes=4 * 2**20),
        name="place",
    )(first[None], *parts, *([] if new else [whole]))


def solution(mesh):
    n_rep = mesh.shape["rep"]
    n_shard = mesh.shape["shard"]
    count = n_shard // n_rep
    middle = n_shard // 2
    order = [p // 2 + p % 2 * middle for p in range(n_shard)]

    def others(pieces):
        pairs = [[((i + j) % n_rep, i) for i in range(n_rep)] for j in range(1, n_rep)]
        return [[lax.ppermute(x, "rep", pair) for x in pieces] for pair in pairs]

    def exchange(pieces, there):
        moved = []
        for j, x in enumerate(pieces):
            pairs = [
                (
                    order[p] * n_rep + r,
                    order[(p + j * n_rep + r) % n_shard] * n_rep + r,
                )
                for p in range(n_shard)
                for r in range(n_rep)
            ]
            pairs = pairs if there else [pair[::-1] for pair in pairs]
            moved.append(lax.ppermute(x, ("shard", "rep"), pairs))
        return moved

    def shards(momentum, gradient):
        experts, rows, cols = momentum.shape
        shard, rep = lax.axis_index("shard"), lax.axis_index("rep")
        place_of = 2 * lax.rem(shard, middle) + shard // middle
        own = exchange(
            blended_share(lax.rem(place_of + rep, n_shard), momentum, gradient, count), True
        )
        rest = others(own)
        momentum, gradient, early = lax.optimization_barrier((momentum, gradient, own[1]))
        new_momentum = new_momentum_of(momentum, gradient)
        own[1] = early
        own[-1], new_momentum = lax.optimization_barrier((own[-1], new_momentum))
        scale = float(max(experts * rows, cols)) ** 0.5
        parts = own + [piece for pieces in rest for piece in pieces]
        update = exchange(orthogonal(parts, count, scale), False)
        whole = (experts, rows, cols)
        for j, pieces in enumerate([update, *others(update)]):
            first = lax.rem(place_of + lax.rem(rep + j, n_rep), n_shard)
            whole = place(first, pieces, whole)
        return new_momentum, whole

    return jax.shard_map(
        shards,
        mesh=mesh,
        in_specs=(P(None, "shard", None), P(None, "shard", None)),
        out_specs=(P(None, "shard", None), P(None, "shard", None)),
        check_vma=False,
    )
```

```python
import functools

import jax
import jax.numpy as jnp
from jax import lax
from jax.experimental import pallas as pl
from jax.experimental.pallas import tpu as pltpu
from jax.sharding import PartitionSpec as P

ITERS = 5

coef_a = 3.4445
coef_b = -4.775
coef_c = 2.0315

LIMIT = 4.0

BF = jnp.bfloat16
F32 = jnp.float32


def next_momentum(m, g):
    return (0.95 * m.astype(F32) + g.astype(F32)).astype(BF)


def blend(m, g):
    return (g.astype(F32) + 0.95 * next_momentum(m, g).astype(F32)).astype(BF)


def distance(core, j, n_rep):
    return j * n_rep + (core + j) % n_rep


def expert(place, core, j, n_rep, experts):
    return lax.rem(place + j * n_rep + lax.rem(core + j, n_rep), experts)


def share_kernel(at_ref, m_hbm, g_hbm, *refs):
    *share_hbms, m_ref, g_ref, share_ref, sems = refs
    count = len(share_hbms)
    experts = m_hbm.shape[0]
    copies = []
    for j in range(count):
        e = expert(at_ref[0], at_ref[1], j, experts // count, experts)
        copies.append(
            [
                pltpu.make_async_copy(src.at[e], dst.at[j], sems.at[i, j])
                for i, (src, dst) in enumerate(((m_hbm, m_ref), (g_hbm, g_ref)))
            ]
        )
        for copy in copies[-1]:
            copy.start()
    for j, share_hbm in enumerate(share_hbms):
        for copy in copies[j]:
            copy.wait()
        share_ref[j] = blend(m_ref[j], g_ref[j])
        copies[j] = pltpu.make_async_copy(share_ref.at[j], share_hbm, sems.at[2, j])
        copies[j].start()
    for copy in copies:
        copy.wait()


def blended_share(at, momentum, gradient, count):
    experts, rows, cols = momentum.shape
    hbm = pl.BlockSpec(memory_space=pltpu.HBM)
    return pl.pallas_call(
        share_kernel,
        in_specs=[pl.BlockSpec(memory_space=pltpu.SMEM), hbm, hbm],
        out_specs=[hbm] * count,
        out_shape=[jax.ShapeDtypeStruct((rows, cols), BF)] * count,
        scratch_shapes=[pltpu.VMEM((count, rows, cols), BF)] * 3
        + [pltpu.SemaphoreType.DMA((3, count))],
        compiler_params=pltpu.CompilerParams(vmem_limit_bytes=60 * 2**20),
        name="share",
    )(at, momentum, gradient)


def momentum_kernel(m_ref, g_ref, new_ref):
    def one(e, carry):
        new_ref[e] = next_momentum(m_ref[e], g_ref[e])
        return carry

    lax.fori_loop(0, m_ref.shape[0], one, 0)


def new_momentum_of(momentum, gradient):
    vmem = pl.BlockSpec(memory_space=pltpu.VMEM)
    return pl.pallas_call(
        momentum_kernel,
        in_specs=[vmem, vmem],
        out_specs=vmem,
        out_shape=jax.ShapeDtypeStruct(momentum.shape, BF),
        cost_estimate=pl.CostEstimate(
            flops=2 * momentum.size, bytes_accessed=6 * momentum.size, transcendentals=0
        ),
        compiler_params=pltpu.CompilerParams(vmem_limit_bytes=16 * 2**20),
        name="new_momentum",
    )(momentum, gradient)


def halves(x):
    high = x.astype(BF)
    return high, (x - high.astype(F32)).astype(BF)


def dot(x, y):
    return jnp.dot(x, y, preferred_element_type=F32)


def dot_transposed(x, y, precision=None):
    return lax.dot_general(
        x, y, (((1,), (1,)), ((), ())), precision=precision, preferred_element_type=F32
    )


def orthogonal_kernel(scale, count, *refs):
    *parts, x_ref, a_ref, s_ref, q_ref = refs[:-6]
    parts, out_refs = parts[:-count], parts[-count:]
    a_left, a_right, m_right, s_left, q_left, full_ref = refs[-6:]
    piece, width = out_refs[0].shape
    height = count * piece
    n = x_ref.shape[0]
    half = n // 2
    for i, part in enumerate(parts):
        x_ref[i * piece : (i + 1) * piece] = part[...]

    def put_out(cols, y):
        for i, out_ref in enumerate(out_refs):
            out_ref[:, cols] = y[i * piece : (i + 1) * piece].astype(BF)

    blocks = ((0, 1), (0, 0), (1, 1))

    def rows(i):
        return slice(i * half, (i + 1) * half)

    def put_left(ref, row, col, high, low):
        height, width = high.shape
        for k, part in enumerate((high, high, low)):
            ref[row : row + height, k * n + col : k * n + col + width] = part

    def put(i, j, x, left=None, right=None):
        for i, j, x in ((i, j, x), (j, i, x.T))[: 1 + (i != j)]:
            high, low = halves(x)
            if left is not None:
                put_left(left, i * half, j * half, high, low)
            if right is not None:
                for k, part in enumerate((high, low, high)):
                    right[k * n + i * half : k * n + (i + 1) * half, rows(j)] = part

    def put_q(q):
        q_ref[...] = q
        high, low = halves(q)
        put_left(q_left, 0, 0, high, low)

    def put_a(i, j, a):
        a_ref[i + j] = a
        put(i, j, a, a_left, a_right)

    eye = lax.broadcasted_iota(jnp.int32, (half, half), 0) == lax.broadcasted_iota(
        jnp.int32, (half, half), 1
    )
    gram = {(i, j): dot_transposed(x_ref[rows(i)], x_ref[rows(j)]) for i, j in blocks}
    square = jnp.sum(jnp.where(eye, gram[0, 0] + gram[1, 1], 0.0), keepdims=True)
    inverse = 1.0 / (jnp.sqrt(square) + 1e-07)
    for i, j in blocks:
        put_a(i, j, gram[i, j] * (inverse * inverse))

    for sweep in range(ITERS - 1):
        for i, j in blocks:
            m = coef_b * a_ref[i + j] + coef_c * dot(a_left[rows(i)], a_right[:, rows(j)])
            put(i, j, m, right=m_right)
            if sweep == 0 and i == 0:
                p = m + jnp.where(eye, coef_a, 0.0) if j == 0 else m
                q_ref[:, rows(j)] = p[:height]
        for i, j in blocks:
            s = coef_a * a_ref[i + j] + dot(a_left[rows(i)], m_right[:, rows(j)])
            s_ref[i + j] = s
            put(i, j, s, left=s_left)
        q = q_ref[...]
        put_q(coef_a * q + dot(q_left[...], m_right[...]) if sweep else q)
        for i, j in blocks:
            put_a(i, j, coef_a * s_ref[i + j] + dot(s_left[rows(i)], m_right[:, rows(j)]))

    q = q_ref[...]
    high, low = halves(coef_b * q + coef_c * dot(q_left[...], a_right[...]))
    put_left(s_left, 0, 0, high, low)
    q = coef_a * q + dot(s_left[:height], a_right[...])
    spread_of_values = jnp.sum(q * q) * (1.0 / (height * n))
    good = spread_of_values < LIMIT

    @pl.when(good)
    def _():
        high, low = halves(q * (inverse * scale))
        q_left[:, :n] = high
        q_left[:, n : 2 * n] = low
        block = min(width, 512)
        for at in range(0, width, block):
            x = x_ref[:, at : at + block]
            y = dot(q_left[:, :n], x) + dot(q_left[:, n : 2 * n], x)
            put_out(slice(at, at + block), y)

    @pl.when(jnp.logical_not(good))
    def _():
        best = lax.Precision.HIGHEST
        block = min(width, 512)

        def columns(i):
            return pl.ds(pl.multiple_of(i * block, block), block)

        def load(i, carry):
            full_ref[:, columns(i)] = x_ref[:, columns(i)].astype(F32) * inverse
            return carry

        def sweep(_, carry):
            def add(i, total):
                x = full_ref[:, columns(i)]
                return total + dot_transposed(x, x, best)

            a = lax.fori_loop(0, width // block, add, jnp.zeros((n, n), F32))
            m = coef_b * a + coef_c * jnp.dot(a, a, precision=best)

            def apply(i, carry):
                x = full_ref[:, columns(i)]
                full_ref[:, columns(i)] = coef_a * x + jnp.dot(m, x, precision=best)
                return carry

            return lax.fori_loop(0, width // block, apply, carry)

        def store(i, carry):
            put_out(columns(i), full_ref[:height, columns(i)] * scale)
            return carry

        lax.fori_loop(0, width // block, load, 0)
        lax.fori_loop(0, ITERS, sweep, 0)
        lax.fori_loop(0, width // block, store, 0)


def orthogonal(parts, count, scale):
    piece, cols = parts[0].shape
    height = piece * count
    n = piece * len(parts)
    vmem = pl.BlockSpec(memory_space=pltpu.VMEM)
    return pl.pallas_call(
        functools.partial(orthogonal_kernel, scale, count),
        in_specs=[vmem] * len(parts),
        out_specs=[vmem] * count,
        out_shape=[jax.ShapeDtypeStruct((piece, cols), BF)] * count,
        scratch_shapes=[
            pltpu.VMEM((n, cols), BF),
            pltpu.VMEM((3, n // 2, n // 2), F32),
            pltpu.VMEM((3, n // 2, n // 2), F32),
            pltpu.VMEM((height, n), F32),
            pltpu.VMEM((n, 3 * n), BF),
            pltpu.VMEM((3 * n, n), BF),
            pltpu.VMEM((3 * n, n), BF),
            pltpu.VMEM((n, 3 * n), BF),
            pltpu.VMEM((height, 3 * n), BF),
            pltpu.VMEM((n, cols), F32),
        ],
        compiler_params=pltpu.CompilerParams(vmem_limit_bytes=40 * 2**20),
        name="orthogonal",
    )(*parts)


def place_kernel(which, n_rep, at_ref, *refs):
    parts, (*_, out_ref, sems) = refs[: len(which)], refs[len(which) :]
    copies = []
    for i, (part, (ahead, j)) in enumerate(zip(parts, which)):
        core = lax.rem(at_ref[1] + ahead, n_rep)
        e = expert(at_ref[0], core, j, n_rep, out_ref.shape[0])
        copies.append(pltpu.make_async_copy(part, out_ref.at[e], sems.at[i]))
        copies[-1].start()
    for copy in copies:
        copy.wait()


def place(at, which, parts, n_rep, whole):
    count = len(parts)
    anywhere = pl.BlockSpec(memory_space=pl.ANY)
    hbm = pl.BlockSpec(memory_space=pltpu.HBM)
    new = isinstance(whole, tuple)
    return pl.pallas_call(
        functools.partial(place_kernel, which, n_rep),
        in_specs=[pl.BlockSpec(memory_space=pltpu.SMEM)] + [anywhere] * count + [hbm] * (not new),
        out_specs=hbm,
        out_shape=jax.ShapeDtypeStruct(whole if new else whole.shape, BF),
        scratch_shapes=[pltpu.SemaphoreType.DMA((count,))],
        input_output_aliases={} if new else {count + 1: 0},
        cost_estimate=pl.CostEstimate(
            flops=0, bytes_accessed=4 * count * parts[0].size, transcendentals=0
        ),
        compiler_params=pltpu.CompilerParams(vmem_limit_bytes=4 * 2**20),
        name="place",
    )(at, *parts, *([] if new else [whole]))


def solution(mesh):
    n_rep = mesh.shape["rep"]
    n_shard = mesh.shape["shard"]
    count = n_shard // n_rep
    middle = n_shard // 2
    order = [p // 2 + p % 2 * middle for p in range(n_shard)]

    def others(pieces):
        pairs = [[((i + j) % n_rep, i) for i in range(n_rep)] for j in range(1, n_rep)]
        return [[lax.ppermute(x, "rep", pair) for x in pieces] for pair in pairs]

    def exchange(pieces, there, first=0):
        moved = []
        for j, x in enumerate(pieces, first):
            pairs = [
                (
                    order[p] * n_rep + r,
                    order[(p + distance(r, j, n_rep)) % n_shard] * n_rep + r,
                )
                for p in range(n_shard)
                for r in range(n_rep)
            ]
            pairs = pairs if there else [pair[::-1] for pair in pairs]
            moved.append(lax.ppermute(x, ("shard", "rep"), pairs))
        return moved

    def shards(momentum, gradient):
        experts, rows, cols = momentum.shape
        shard, rep = lax.axis_index("shard"), lax.axis_index("rep")
        at = jnp.stack([2 * lax.rem(shard, middle) + shard // middle, rep])
        sent = blended_share(at, momentum, gradient, count)
        late = count // 4
        own = exchange(sent[:-late], True)
        momentum, gradient, own[0] = lax.optimization_barrier((momentum, gradient, own[0]))
        new_momentum = new_momentum_of(momentum, gradient)
        last, new_momentum = lax.optimization_barrier((sent[-late:], new_momentum))
        own += exchange(last, True, count - late)
        scale = float(max(experts * rows, cols)) ** 0.5
        parts = own + [piece for pieces in others(own) for piece in pieces]
        update = exchange(orthogonal(parts, count, scale), False)
        pieces = {(i, j): x for i, xs in enumerate([update, *others(update)]) for j, x in enumerate(xs)}
        early = [(i, j) for i, j in pieces if j < (count // 2 if i else 3 * count // 4)]
        whole = (experts, rows, cols)
        for which in (early, [key for key in pieces if key not in early]):
            whole = place(at, which, [pieces[key] for key in which], n_rep, whole)
        return new_momentum, whole

    return jax.shard_map(
        shards,
        mesh=mesh,
        in_specs=(P(None, "shard", None), P(None, "shard", None)),
        out_specs=(P(None, "shard", None), P(None, "shard", None)),
        check_vma=False,
    )
```

```python
import functools

import jax
import jax.numpy as jnp
from jax import lax
from jax.experimental import pallas as pl
from jax.experimental.pallas import tpu as pltpu
from jax.sharding import PartitionSpec as P

ITERS = 5

coef_a = 3.4445
coef_b = -4.775
coef_c = 2.0315

LIMIT = 4.0

BF = jnp.bfloat16
F32 = jnp.float32


def next_momentum(m, g):
    return (0.95 * m.astype(F32) + g.astype(F32)).astype(BF)


def blend(m, g):
    return (g.astype(F32) + 0.95 * next_momentum(m, g).astype(F32)).astype(BF)


def share_kernel(n_rep, at_ref, m_hbm, g_hbm, *refs):
    *share_hbms, m_ref, g_ref, share_ref, sems = refs
    count = len(share_hbms)
    experts = m_hbm.shape[0]
    copies = []
    for j in range(count):
        e = lax.rem(at_ref[0] + j * n_rep, experts)
        copies.append(
            [
                pltpu.make_async_copy(src.at[e], dst.at[j], sems.at[i, j])
                for i, (src, dst) in enumerate(((m_hbm, m_ref), (g_hbm, g_ref)))
            ]
        )
        for copy in copies[-1]:
            copy.start()
    for j, share_hbm in enumerate(share_hbms):
        for copy in copies[j]:
            copy.wait()
        share_ref[j] = blend(m_ref[j], g_ref[j])
        copies[j] = pltpu.make_async_copy(share_ref.at[j], share_hbm, sems.at[2, j])
        copies[j].start()
    for copy in copies:
        copy.wait()


def blended_share(first, momentum, gradient, count, n_rep):
    experts, rows, cols = momentum.shape
    hbm = pl.BlockSpec(memory_space=pltpu.HBM)
    return pl.pallas_call(
        functools.partial(share_kernel, n_rep),
        in_specs=[pl.BlockSpec(memory_space=pltpu.SMEM), hbm, hbm],
        out_specs=[hbm] * count,
        out_shape=[jax.ShapeDtypeStruct((rows, cols), BF)] * count,
        scratch_shapes=[pltpu.VMEM((count, rows, cols), BF)] * 3
        + [pltpu.SemaphoreType.DMA((3, count))],
        compiler_params=pltpu.CompilerParams(vmem_limit_bytes=60 * 2**20),
        name="share",
    )(first[None], momentum, gradient)


def momentum_kernel(m_ref, g_ref, new_ref):
    def one(e, carry):
        new_ref[e] = next_momentum(m_ref[e], g_ref[e])
        return carry

    lax.fori_loop(0, m_ref.shape[0], one, 0)


def new_momentum_of(momentum, gradient):
    vmem = pl.BlockSpec(memory_space=pltpu.VMEM)
    return pl.pallas_call(
        momentum_kernel,
        in_specs=[vmem, vmem],
        out_specs=vmem,
        out_shape=jax.ShapeDtypeStruct(momentum.shape, BF),
        cost_estimate=pl.CostEstimate(
            flops=2 * momentum.size, bytes_accessed=6 * momentum.size, transcendentals=0
        ),
        compiler_params=pltpu.CompilerParams(vmem_limit_bytes=16 * 2**20),
        name="new_momentum",
    )(momentum, gradient)


def halves(x):
    high = x.astype(BF)
    return high, (x - high.astype(F32)).astype(BF)


def dot(x, y):
    return jnp.dot(x, y, preferred_element_type=F32)


def dot_transposed(x, y, precision=None):
    return lax.dot_general(
        x, y, (((1,), (1,)), ((), ())), precision=precision, preferred_element_type=F32
    )


def orthogonal_kernel(scale, count, *refs):
    *parts, x_ref, a_ref, s_ref, q_ref = refs[:-6]
    parts, out_refs = parts[:-count], parts[-count:]
    a_left, a_right, m_right, s_left, q_left, full_ref = refs[-6:]
    piece, width = out_refs[0].shape
    height = count * piece
    n = x_ref.shape[0]
    half = n // 2
    for i, part in enumerate(parts):
        x_ref[i * piece : (i + 1) * piece] = part[...]

    def put_out(cols, y):
        for i, out_ref in enumerate(out_refs):
            out_ref[:, cols] = y[i * piece : (i + 1) * piece].astype(BF)

    blocks = ((0, 1), (0, 0), (1, 1))

    def rows(i):
        return slice(i * half, (i + 1) * half)

    def put_left(ref, row, col, high, low):
        height, width = high.shape
        for k, part in enumerate((high, high, low)):
            ref[row : row + height, k * n + col : k * n + col + width] = part

    def put(i, j, x, left=None, right=None):
        for i, j, x in ((i, j, x), (j, i, x.T))[: 1 + (i != j)]:
            high, low = halves(x)
            if left is not None:
                put_left(left, i * half, j * half, high, low)
            if right is not None:
                for k, part in enumerate((high, low, high)):
                    right[k * n + i * half : k * n + (i + 1) * half, rows(j)] = part

    def put_q(q):
        q_ref[...] = q
        high, low = halves(q)
        put_left(q_left, 0, 0, high, low)

    def put_a(i, j, a):
        a_ref[i + j] = a
        put(i, j, a, a_left, a_right)

    eye = lax.broadcasted_iota(jnp.int32, (half, half), 0) == lax.broadcasted_iota(
        jnp.int32, (half, half), 1
    )
    gram = {(i, j): dot_transposed(x_ref[rows(i)], x_ref[rows(j)]) for i, j in blocks}
    square = jnp.sum(jnp.where(eye, gram[0, 0] + gram[1, 1], 0.0), keepdims=True)
    inverse = 1.0 / (jnp.sqrt(square) + 1e-07)
    for i, j in blocks:
        put_a(i, j, gram[i, j] * (inverse * inverse))

    for sweep in range(ITERS - 1):
        for i, j in blocks:
            m = coef_b * a_ref[i + j] + coef_c * dot(a_left[rows(i)], a_right[:, rows(j)])
            put(i, j, m, right=m_right)
            if sweep == 0 and i == 0:
                p = m + jnp.where(eye, coef_a, 0.0) if j == 0 else m
                q_ref[:, rows(j)] = p[:height]
        for i, j in blocks:
            s = coef_a * a_ref[i + j] + dot(a_left[rows(i)], m_right[:, rows(j)])
            s_ref[i + j] = s
            put(i, j, s, left=s_left)
        q = q_ref[...]
        put_q(coef_a * q + dot(q_left[...], m_right[...]) if sweep else q)
        for i, j in blocks:
            put_a(i, j, coef_a * s_ref[i + j] + dot(s_left[rows(i)], m_right[:, rows(j)]))

    q = q_ref[...]
    high, low = halves(coef_b * q + coef_c * dot(q_left[...], a_right[...]))
    put_left(s_left, 0, 0, high, low)
    q = coef_a * q + dot(s_left[:height], a_right[...])
    spread_of_values = jnp.sum(q * q) * (1.0 / (height * n))
    good = spread_of_values < LIMIT

    @pl.when(good)
    def _():
        high, low = halves(q * (inverse * scale))
        q_left[:, :n] = high
        q_left[:, n : 2 * n] = low
        block = min(width, 512)
        for at in range(0, width, block):
            x = x_ref[:, at : at + block]
            y = dot(q_left[:, :n], x) + dot(q_left[:, n : 2 * n], x)
            put_out(slice(at, at + block), y)

    @pl.when(jnp.logical_not(good))
    def _():
        best = lax.Precision.HIGHEST
        block = min(width, 512)

        def columns(i):
            return pl.ds(pl.multiple_of(i * block, block), block)

        def load(i, carry):
            full_ref[:, columns(i)] = x_ref[:, columns(i)].astype(F32) * inverse
            return carry

        def sweep(_, carry):
            def add(i, total):
                x = full_ref[:, columns(i)]
                return total + dot_transposed(x, x, best)

            a = lax.fori_loop(0, width // block, add, jnp.zeros((n, n), F32))
            m = coef_b * a + coef_c * jnp.dot(a, a, precision=best)

            def apply(i, carry):
                x = full_ref[:, columns(i)]
                full_ref[:, columns(i)] = coef_a * x + jnp.dot(m, x, precision=best)
                return carry

            return lax.fori_loop(0, width // block, apply, carry)

        def store(i, carry):
            put_out(columns(i), full_ref[:height, columns(i)] * scale)
            return carry

        lax.fori_loop(0, width // block, load, 0)
        lax.fori_loop(0, ITERS, sweep, 0)
        lax.fori_loop(0, width // block, store, 0)


def orthogonal(parts, count, scale):
    piece, cols = parts[0].shape
    height = piece * count
    n = piece * len(parts)
    vmem = pl.BlockSpec(memory_space=pltpu.VMEM)
    return pl.pallas_call(
        functools.partial(orthogonal_kernel, scale, count),
        in_specs=[vmem] * len(parts),
        out_specs=[vmem] * count,
        out_shape=[jax.ShapeDtypeStruct((piece, cols), BF)] * count,
        scratch_shapes=[
            pltpu.VMEM((n, cols), BF),
            pltpu.VMEM((3, n // 2, n // 2), F32),
            pltpu.VMEM((3, n // 2, n // 2), F32),
            pltpu.VMEM((height, n), F32),
            pltpu.VMEM((n, 3 * n), BF),
            pltpu.VMEM((3 * n, n), BF),
            pltpu.VMEM((3 * n, n), BF),
            pltpu.VMEM((n, 3 * n), BF),
            pltpu.VMEM((height, 3 * n), BF),
            pltpu.VMEM((n, cols), F32),
        ],
        compiler_params=pltpu.CompilerParams(vmem_limit_bytes=40 * 2**20),
        name="orthogonal",
    )(*parts)


def place_kernel(which, n_rep, at_ref, *refs):
    parts, (*_, out_ref, sems) = refs[: len(which)], refs[len(which) :]
    copies = []
    for i, (part, (ahead, j)) in enumerate(zip(parts, which)):
        e = lax.rem(at_ref[ahead] + j * n_rep, out_ref.shape[0])
        copies.append(pltpu.make_async_copy(part, out_ref.at[e], sems.at[i]))
        copies[-1].start()
    for copy in copies:
        copy.wait()


def place(firsts, pieces, n_rep, whole):
    count = len(pieces)
    anywhere = pl.BlockSpec(memory_space=pl.ANY)
    hbm = pl.BlockSpec(memory_space=pltpu.HBM)
    new = isinstance(whole, tuple)
    parts = list(pieces.values())
    return pl.pallas_call(
        functools.partial(place_kernel, list(pieces), n_rep),
        in_specs=[pl.BlockSpec(memory_space=pltpu.SMEM)] + [anywhere] * count + [hbm] * (not new),
        out_specs=hbm,
        out_shape=jax.ShapeDtypeStruct(whole if new else whole.shape, BF),
        scratch_shapes=[pltpu.SemaphoreType.DMA((count,))],
        input_output_aliases={} if new else {count + 1: 0},
        cost_estimate=pl.CostEstimate(
            flops=0, bytes_accessed=4 * count * parts[0].size, transcendentals=0
        ),
        compiler_params=pltpu.CompilerParams(vmem_limit_bytes=4 * 2**20),
        name="place",
    )(firsts, *parts, *([] if new else [whole]))


def solution(mesh):
    n_rep = mesh.shape["rep"]
    n_shard = mesh.shape["shard"]
    count = n_shard // n_rep
    middle = n_shard // 2
    order = [p // 2 + p % 2 * middle for p in range(n_shard)]

    def others(pieces):
        pairs = [[((i + j) % n_rep, i) for i in range(n_rep)] for j in range(1, n_rep)]
        return [[lax.ppermute(x, "rep", pair) for x in pieces] for pair in pairs]

    def exchange(pieces, there):
        moved = []
        for j, x in enumerate(pieces):
            pairs = [
                (
                    order[p] * n_rep + r,
                    order[(p + j * n_rep + r) % n_shard] * n_rep + r,
                )
                for p in range(n_shard)
                for r in range(n_rep)
            ]
            pairs = pairs if there else [pair[::-1] for pair in pairs]
            moved.append(lax.ppermute(x, ("shard", "rep"), pairs))
        return moved

    def after(x, y):
        return lax.optimization_barrier((x, y))[0]

    def shards(momentum, gradient):
        experts, rows, cols = momentum.shape
        shard, rep = lax.axis_index("shard"), lax.axis_index("rep")
        place_of = 2 * lax.rem(shard, middle) + shard // middle
        first = lax.rem(place_of + rep, n_shard)
        few = count // 4
        own = exchange(blended_share(first, momentum, gradient, count, n_rep), True)

        middle_piece = (count - 1) // 2
        momentum, gradient, own[middle_piece] = lax.optimization_barrier(
            (momentum, gradient, own[middle_piece])
        )
        new_momentum = new_momentum_of(momentum, gradient)
        own = [after(x, new_momentum) for x in own]
        scale = float(max(experts * rows, cols)) ** 0.5
        parts = own + [piece for pieces in others(own) for piece in pieces]
        update = exchange(orthogonal(parts, count, scale), False)

        firsts = jnp.stack(
            [lax.rem(place_of + lax.rem(rep + i, n_rep), n_shard) for i in range(n_rep)]
        )
        early = count - few
        whole = place(
            firsts, {(0, j): update[j] for j in range(early)}, n_rep, (experts, rows, cols)
        )
        update[early:] = [after(x, whole) for x in update[early:]]
        swapped = others(update)
        whole = place(
            firsts,
            {(0, j): update[j] for j in range(early, count)}
            | {(i, j): x for i, xs in enumerate(swapped, 1) for j, x in enumerate(xs[:early])},
            n_rep,
            whole,
        )
        whole = place(
            firsts,
            {(i, j): xs[j] for i, xs in enumerate(swapped, 1) for j in range(early, count)},
            n_rep,
            whole,
        )
        return new_momentum, whole

    return jax.shard_map(
        shards,
        mesh=mesh,
        in_specs=(P(None, "shard", None), P(None, "shard", None)),
        out_specs=(P(None, "shard", None), P(None, "shard", None)),
        check_vma=False,
    )
```

```python
import functools

import jax
import jax.numpy as jnp
from jax import lax
from jax.experimental import pallas as pl
from jax.experimental.pallas import tpu as pltpu
from jax.sharding import PartitionSpec as P

ITERS = 5

coef_a = 3.4445
coef_b = -4.775
coef_c = 2.0315

LIMIT = 4.0

BF = jnp.bfloat16
F32 = jnp.float32


def next_momentum(m, g):
    return (0.95 * m.astype(F32) + g.astype(F32)).astype(BF)


def blend(m, g):
    return (g.astype(F32) + 0.95 * next_momentum(m, g).astype(F32)).astype(BF)


def share_kernel(n_rep, at_ref, m_hbm, g_hbm, *refs):
    *share_hbms, m_ref, g_ref, share_ref, sems = refs
    count = len(share_hbms)
    experts = m_hbm.shape[0]
    copies = []
    for j in range(count):
        e = lax.rem(at_ref[0] + j * n_rep, experts)
        copies.append(
            [
                pltpu.make_async_copy(src.at[e], dst.at[j], sems.at[i, j])
                for i, (src, dst) in enumerate(((m_hbm, m_ref), (g_hbm, g_ref)))
            ]
        )
        for copy in copies[-1]:
            copy.start()
    for j, share_hbm in enumerate(share_hbms):
        for copy in copies[j]:
            copy.wait()
        share_ref[j] = blend(m_ref[j], g_ref[j])
        copies[j] = pltpu.make_async_copy(share_ref.at[j], share_hbm, sems.at[2, j])
        copies[j].start()
    for copy in copies:
        copy.wait()


def blended_share(first, momentum, gradient, count, n_rep):
    experts, rows, cols = momentum.shape
    hbm = pl.BlockSpec(memory_space=pltpu.HBM)
    return pl.pallas_call(
        functools.partial(share_kernel, n_rep),
        in_specs=[pl.BlockSpec(memory_space=pltpu.SMEM), hbm, hbm],
        out_specs=[hbm] * count,
        out_shape=[jax.ShapeDtypeStruct((rows, cols), BF)] * count,
        scratch_shapes=[pltpu.VMEM((count, rows, cols), BF)] * 3
        + [pltpu.SemaphoreType.DMA((3, count))],
        compiler_params=pltpu.CompilerParams(vmem_limit_bytes=60 * 2**20),
        name="share",
    )(first[None], momentum, gradient)


def momentum_kernel(m_ref, g_ref, new_ref):
    def one(e, carry):
        new_ref[e] = next_momentum(m_ref[e], g_ref[e])
        return carry

    lax.fori_loop(0, m_ref.shape[0], one, 0)


def new_momentum_of(momentum, gradient):
    vmem = pl.BlockSpec(memory_space=pltpu.VMEM)
    return pl.pallas_call(
        momentum_kernel,
        in_specs=[vmem, vmem],
        out_specs=vmem,
        out_shape=jax.ShapeDtypeStruct(momentum.shape, BF),
        cost_estimate=pl.CostEstimate(
            flops=2 * momentum.size, bytes_accessed=6 * momentum.size, transcendentals=0
        ),
        compiler_params=pltpu.CompilerParams(vmem_limit_bytes=16 * 2**20),
        name="new_momentum",
    )(momentum, gradient)


def halves(x):
    high = x.astype(BF)
    return high, (x - high.astype(F32)).astype(BF)


def dot(x, y):
    return jnp.dot(x, y, preferred_element_type=F32)


def dot_transposed(x, y, precision=None):
    return lax.dot_general(
        x, y, (((1,), (1,)), ((), ())), precision=precision, preferred_element_type=F32
    )


def orthogonal_kernel(scale, count, *refs):
    *parts, x_ref, a_ref, s_ref, q_ref = refs[:-6]
    parts, out_refs = parts[:-count], parts[-count:]
    a_left, a_right, m_right, s_left, q_left, full_ref = refs[-6:]
    piece, width = out_refs[0].shape
    height = count * piece
    n = x_ref.shape[0]
    half = n // 2
    at = 0
    for part in parts:
        x_ref[at : at + part.shape[0]] = part[...]
        at += part.shape[0]

    def put_out(cols, y):
        for i, out_ref in enumerate(out_refs):
            out_ref[:, cols] = y[i * piece : (i + 1) * piece].astype(BF)

    blocks = ((0, 1), (0, 0), (1, 1))

    def rows(i):
        return slice(i * half, (i + 1) * half)

    def put_left(ref, row, col, high, low):
        height, width = high.shape
        for k, part in enumerate((high, high, low)):
            ref[row : row + height, k * n + col : k * n + col + width] = part

    def put(i, j, x, left=None, right=None):
        for i, j, x in ((i, j, x), (j, i, x.T))[: 1 + (i != j)]:
            high, low = halves(x)
            if left is not None:
                put_left(left, i * half, j * half, high, low)
            if right is not None:
                for k, part in enumerate((high, low, high)):
                    right[k * n + i * half : k * n + (i + 1) * half, rows(j)] = part

    def put_q(q):
        q_ref[...] = q
        high, low = halves(q)
        put_left(q_left, 0, 0, high, low)

    def put_a(i, j, a):
        a_ref[i + j] = a
        put(i, j, a, a_left, a_right)

    eye = lax.broadcasted_iota(jnp.int32, (half, half), 0) == lax.broadcasted_iota(
        jnp.int32, (half, half), 1
    )
    gram = {(i, j): dot_transposed(x_ref[rows(i)], x_ref[rows(j)]) for i, j in blocks}
    square = jnp.sum(jnp.where(eye, gram[0, 0] + gram[1, 1], 0.0), keepdims=True)
    inverse = 1.0 / (jnp.sqrt(square) + 1e-07)
    for i, j in blocks:
        put_a(i, j, gram[i, j] * (inverse * inverse))

    for sweep in range(ITERS - 1):
        for i, j in blocks:
            m = coef_b * a_ref[i + j] + coef_c * dot(a_left[rows(i)], a_right[:, rows(j)])
            put(i, j, m, right=m_right)
            if sweep == 0 and i == 0:
                p = m + jnp.where(eye, coef_a, 0.0) if j == 0 else m
                q_ref[:, rows(j)] = p[:height]
        for i, j in blocks:
            s = coef_a * a_ref[i + j] + dot(a_left[rows(i)], m_right[:, rows(j)])
            s_ref[i + j] = s
            put(i, j, s, left=s_left)
        q = q_ref[...]
        put_q(coef_a * q + dot(q_left[...], m_right[...]) if sweep else q)
        for i, j in blocks:
            put_a(i, j, coef_a * s_ref[i + j] + dot(s_left[rows(i)], m_right[:, rows(j)]))

    q = q_ref[...]
    high, low = halves(coef_b * q + coef_c * dot(q_left[...], a_right[...]))
    put_left(s_left, 0, 0, high, low)
    q = coef_a * q + dot(s_left[:height], a_right[...])
    spread_of_values = jnp.sum(q * q) * (1.0 / (height * n))
    good = spread_of_values < LIMIT

    @pl.when(good)
    def _():
        high, low = halves(q * (inverse * scale))
        q_left[:, :n] = high
        q_left[:, n : 2 * n] = low
        block = min(width, 512)
        for at in range(0, width, block):
            x = x_ref[:, at : at + block]
            y = dot(q_left[:, :n], x) + dot(q_left[:, n : 2 * n], x)
            put_out(slice(at, at + block), y)

    @pl.when(jnp.logical_not(good))
    def _():
        best = lax.Precision.HIGHEST
        block = min(width, 512)

        def columns(i):
            return pl.ds(pl.multiple_of(i * block, block), block)

        def load(i, carry):
            full_ref[:, columns(i)] = x_ref[:, columns(i)].astype(F32) * inverse
            return carry

        def sweep(_, carry):
            def add(i, total):
                x = full_ref[:, columns(i)]
                return total + dot_transposed(x, x, best)

            a = lax.fori_loop(0, width // block, add, jnp.zeros((n, n), F32))
            m = coef_b * a + coef_c * jnp.dot(a, a, precision=best)

            def apply(i, carry):
                x = full_ref[:, columns(i)]
                full_ref[:, columns(i)] = coef_a * x + jnp.dot(m, x, precision=best)
                return carry

            return lax.fori_loop(0, width // block, apply, carry)

        def store(i, carry):
            put_out(columns(i), full_ref[:height, columns(i)] * scale)
            return carry

        lax.fori_loop(0, width // block, load, 0)
        lax.fori_loop(0, ITERS, sweep, 0)
        lax.fori_loop(0, width // block, store, 0)


def orthogonal(parts, count, scale):
    piece, cols = parts[0].shape
    height = piece * count
    n = sum(part.shape[0] for part in parts)
    vmem = pl.BlockSpec(memory_space=pltpu.VMEM)
    return pl.pallas_call(
        functools.partial(orthogonal_kernel, scale, count),
        in_specs=[vmem] * len(parts),
        out_specs=[vmem] * count,
        out_shape=[jax.ShapeDtypeStruct((piece, cols), BF)] * count,
        scratch_shapes=[
            pltpu.VMEM((n, cols), BF),
            pltpu.VMEM((3, n // 2, n // 2), F32),
            pltpu.VMEM((3, n // 2, n // 2), F32),
            pltpu.VMEM((height, n), F32),
            pltpu.VMEM((n, 3 * n), BF),
            pltpu.VMEM((3 * n, n), BF),
            pltpu.VMEM((3 * n, n), BF),
            pltpu.VMEM((n, 3 * n), BF),
            pltpu.VMEM((height, 3 * n), BF),
            pltpu.VMEM((n, cols), F32),
        ],
        compiler_params=pltpu.CompilerParams(vmem_limit_bytes=40 * 2**20),
        name="orthogonal",
    )(*parts)


def place_kernel(which, n_rep, *refs):
    aheads = sorted({ahead for names in which for ahead, _ in names})
    firsts = dict(zip(aheads, refs))
    parts, (*_, out_ref, sems) = refs[len(aheads) :][: len(which)], refs[len(aheads) + len(which) :]
    rows = out_ref.shape[1]
    copies = []
    for part, names in zip(parts, which):
        for i, (ahead, j) in enumerate(names):
            e = lax.rem(firsts[ahead][0] + j * n_rep, out_ref.shape[0])
            src = part.at[pl.ds(i * rows, rows)]
            copies.append(pltpu.make_async_copy(src, out_ref.at[e], sems.at[len(copies)]))
            copies[-1].start()
    for copy in copies:
        copy.wait()


def place(firsts, which, parts, n_rep, whole):
    count = sum(len(names) for names in which)
    indices = [firsts[i] for i in sorted({ahead for names in which for ahead, _ in names})]
    hbm = pl.BlockSpec(memory_space=pltpu.HBM)
    new = isinstance(whole, tuple)
    return pl.pallas_call(
        functools.partial(place_kernel, which, n_rep),
        in_specs=[pl.BlockSpec(memory_space=pltpu.SMEM)] * len(indices)
        + [pl.BlockSpec(memory_space=pl.ANY)] * len(parts)
        + [hbm] * (not new),
        out_specs=hbm,
        out_shape=jax.ShapeDtypeStruct(whole if new else whole.shape, BF),
        scratch_shapes=[pltpu.SemaphoreType.DMA((count,))],
        input_output_aliases={} if new else {len(indices) + len(parts): 0},
        cost_estimate=pl.CostEstimate(
            flops=0, bytes_accessed=4 * sum(x.size for x in parts), transcendentals=0
        ),
        compiler_params=pltpu.CompilerParams(vmem_limit_bytes=4 * 2**20),
        name="place",
    )(*indices, *parts, *([] if new else [whole]))


def solution(mesh):
    n_rep = mesh.shape["rep"]
    n_shard = mesh.shape["shard"]
    count = n_shard // n_rep
    middle = n_shard // 2
    order = [p // 2 + p % 2 * middle for p in range(n_shard)]

    def others(pieces):
        pairs = [[((i + j) % n_rep, i) for i in range(n_rep)] for j in range(1, n_rep)]
        return [[lax.ppermute(x, "rep", pair) for x in pieces] for pair in pairs]

    def exchange(pieces, there):
        moved = []
        for j, x in enumerate(pieces):
            pairs = [
                (
                    order[p] * n_rep + r,
                    order[(p + j * n_rep + r) % n_shard] * n_rep + r,
                )
                for p in range(n_shard)
                for r in range(n_rep)
            ]
            pairs = pairs if there else [pair[::-1] for pair in pairs]
            moved.append(lax.ppermute(x, ("shard", "rep"), pairs))
        return moved

    def after(x, y):
        return lax.optimization_barrier((x, y))[0]

    def shards(momentum, gradient):
        experts, rows, cols = momentum.shape
        shard, rep = lax.axis_index("shard"), lax.axis_index("rep")
        place_of = 2 * lax.rem(shard, middle) + shard // middle
        first = lax.rem(place_of + rep, n_shard)
        few = count // 4
        own = exchange(blended_share(first, momentum, gradient, count, n_rep), True)

        middle_piece = (count - 1) // 2
        momentum, gradient, own[middle_piece] = lax.optimization_barrier(
            (momentum, gradient, own[middle_piece])
        )
        new_momentum = new_momentum_of(momentum, gradient)
        own = [after(x, new_momentum) for x in own]

        scale = float(max(experts * rows, cols)) ** 0.5
        parts = own + [x for xs in others(own) for x in xs]
        update = exchange(orthogonal(parts, count, scale), False)

        firsts = [lax.rem(place_of + lax.rem(rep + i, n_rep), n_shard)[None] for i in range(n_rep)]
        early = count - few
        soon = 3 * count // 8
        whole = place(
            firsts, [[(0, j)] for j in range(early)], update[:early], n_rep, (experts, rows, cols)
        )
        update[early:] = [after(x, whole) for x in update[early:]]
        swapped = others(update)
        second = [(0, j) for j in range(early, count)]
        second += [(i, j) for i in range(1, n_rep) for j in range(soon)]
        third = [(i, j) for i in range(1, n_rep) for j in range(soon, count)]
        for names in (second, third):
            pieces = [swapped[i - 1][j] if i else update[j] for i, j in names]
            whole = place(firsts, [[name] for name in names], pieces, n_rep, whole)
        return new_momentum, whole

    return jax.shard_map(
        shards,
        mesh=mesh,
        in_specs=(P(None, "shard", None), P(None, "shard", None)),
        out_specs=(P(None, "shard", None), P(None, "shard", None)),
        check_vma=False,
    )
```

```python
import functools

import jax
import jax.numpy as jnp
from jax import lax
from jax.experimental import pallas as pl
from jax.experimental.pallas import tpu as pltpu
from jax.sharding import PartitionSpec as P

ITERS = 5

coef_a = 3.4445
coef_b = -4.775
coef_c = 2.0315

LIMIT = 4.0

BF = jnp.bfloat16
F32 = jnp.float32


def next_momentum(m, g):
    return (0.95 * m.astype(F32) + g.astype(F32)).astype(BF)


def blend(m, g):
    return (g.astype(F32) + 0.95 * next_momentum(m, g).astype(F32)).astype(BF)


def share_kernel(n_rep, at_ref, m_hbm, g_hbm, *refs):
    *share_hbms, m_ref, g_ref, share_ref, sems = refs
    count = len(share_hbms)
    experts = m_hbm.shape[0]
    copies = []
    for j in range(count):
        e = lax.rem(at_ref[0] + j * n_rep, experts)
        copies.append(
            [
                pltpu.make_async_copy(src.at[e], dst.at[j], sems.at[i, j])
                for i, (src, dst) in enumerate(((m_hbm, m_ref), (g_hbm, g_ref)))
            ]
        )
        for copy in copies[-1]:
            copy.start()
    for j, share_hbm in enumerate(share_hbms):
        for copy in copies[j]:
            copy.wait()
        share_ref[j] = blend(m_ref[j], g_ref[j])
        copies[j] = pltpu.make_async_copy(share_ref.at[j], share_hbm, sems.at[2, j])
        copies[j].start()
    for copy in copies:
        copy.wait()


def blended_share(first, momentum, gradient, count, n_rep):
    experts, rows, cols = momentum.shape
    hbm = pl.BlockSpec(memory_space=pltpu.HBM)
    return pl.pallas_call(
        functools.partial(share_kernel, n_rep),
        in_specs=[pl.BlockSpec(memory_space=pltpu.SMEM), hbm, hbm],
        out_specs=[hbm] * count,
        out_shape=[jax.ShapeDtypeStruct((rows, cols), BF)] * count,
        scratch_shapes=[pltpu.VMEM((count, rows, cols), BF)] * 3
        + [pltpu.SemaphoreType.DMA((3, count))],
        compiler_params=pltpu.CompilerParams(vmem_limit_bytes=60 * 2**20),
        name="share",
    )(first[None], momentum, gradient)


def momentum_kernel(m_ref, g_ref, new_ref):
    def one(e, carry):
        new_ref[e] = next_momentum(m_ref[e], g_ref[e])
        return carry

    lax.fori_loop(0, m_ref.shape[0], one, 0)


def new_momentum_of(momentum, gradient):
    vmem = pl.BlockSpec(memory_space=pltpu.VMEM)
    return pl.pallas_call(
        momentum_kernel,
        in_specs=[vmem, vmem],
        out_specs=vmem,
        out_shape=jax.ShapeDtypeStruct(momentum.shape, BF),
        cost_estimate=pl.CostEstimate(
            flops=2 * momentum.size, bytes_accessed=6 * momentum.size, transcendentals=0
        ),
        compiler_params=pltpu.CompilerParams(vmem_limit_bytes=16 * 2**20),
        name="new_momentum",
    )(momentum, gradient)


def halves(x):
    high = x.astype(BF)
    return high, (x - high.astype(F32)).astype(BF)


def dot(x, y):
    return jnp.dot(x, y, preferred_element_type=F32)


def dot_transposed(x, y, precision=None):
    return lax.dot_general(
        x, y, (((1,), (1,)), ((), ())), precision=precision, preferred_element_type=F32
    )


def orthogonal_kernel(scale, count, *refs):
    *parts, x_ref, a_ref, s_ref, q_ref = refs[:-6]
    parts, out_refs = parts[:-count], parts[-count:]
    a_left, a_right, m_right, s_left, q_left, full_ref = refs[-6:]
    piece, width = out_refs[0].shape
    height = count * piece
    n = x_ref.shape[0]
    half = n // 2
    at = 0
    for part in parts:
        x_ref[at : at + part.shape[0]] = part[...]
        at += part.shape[0]

    def put_out(cols, y):
        for i, out_ref in enumerate(out_refs):
            out_ref[:, cols] = y[i * piece : (i + 1) * piece].astype(BF)

    blocks = ((0, 1), (0, 0), (1, 1))

    def rows(i):
        return slice(i * half, (i + 1) * half)

    def put_left(ref, row, col, high, low):
        height, width = high.shape
        for k, part in enumerate((high, high, low)):
            ref[row : row + height, k * n + col : k * n + col + width] = part

    def put(i, j, x, left=None, right=None):
        for i, j, x in ((i, j, x), (j, i, x.T))[: 1 + (i != j)]:
            high, low = halves(x)
            if left is not None:
                put_left(left, i * half, j * half, high, low)
            if right is not None:
                for k, part in enumerate((high, low, high)):
                    right[k * n + i * half : k * n + (i + 1) * half, rows(j)] = part

    def put_q(q):
        q_ref[...] = q
        high, low = halves(q)
        put_left(q_left, 0, 0, high, low)

    def put_a(i, j, a):
        a_ref[i + j] = a
        put(i, j, a, a_left, a_right)

    eye = lax.broadcasted_iota(jnp.int32, (half, half), 0) == lax.broadcasted_iota(
        jnp.int32, (half, half), 1
    )
    gram = {(i, j): dot_transposed(x_ref[rows(i)], x_ref[rows(j)]) for i, j in blocks}
    square = jnp.sum(jnp.where(eye, gram[0, 0] + gram[1, 1], 0.0), keepdims=True)
    inverse = 1.0 / (jnp.sqrt(square) + 1e-07)
    for i, j in blocks:
        put_a(i, j, gram[i, j] * (inverse * inverse))

    for sweep in range(ITERS - 1):
        for i, j in blocks:
            m = coef_b * a_ref[i + j] + coef_c * dot(a_left[rows(i)], a_right[:, rows(j)])
            put(i, j, m, right=m_right)
            if sweep == 0 and i == 0:
                p = m + jnp.where(eye, coef_a, 0.0) if j == 0 else m
                q_ref[:, rows(j)] = p[:height]
        for i, j in blocks:
            s = coef_a * a_ref[i + j] + dot(a_left[rows(i)], m_right[:, rows(j)])
            s_ref[i + j] = s
            put(i, j, s, left=s_left)
        q = q_ref[...]
        put_q(coef_a * q + dot(q_left[...], m_right[...]) if sweep else q)
        for i, j in blocks:
            put_a(i, j, coef_a * s_ref[i + j] + dot(s_left[rows(i)], m_right[:, rows(j)]))

    q = q_ref[...]
    high, low = halves(coef_b * q + coef_c * dot(q_left[...], a_right[...]))
    put_left(s_left, 0, 0, high, low)
    q = coef_a * q + dot(s_left[:height], a_right[...])
    spread_of_values = jnp.sum(q * q) * (1.0 / (height * n))
    good = spread_of_values < LIMIT

    @pl.when(good)
    def _():
        high, low = halves(q * (inverse * scale))
        q_left[:, :n] = high
        q_left[:, n : 2 * n] = low
        block = min(width, 512)
        for at in range(0, width, block):
            x = x_ref[:, at : at + block]
            y = dot(q_left[:, :n], x) + dot(q_left[:, n : 2 * n], x)
            put_out(slice(at, at + block), y)

    @pl.when(jnp.logical_not(good))
    def _():
        best = lax.Precision.HIGHEST
        block = min(width, 512)

        def columns(i):
            return pl.ds(pl.multiple_of(i * block, block), block)

        def load(i, carry):
            full_ref[:, columns(i)] = x_ref[:, columns(i)].astype(F32) * inverse
            return carry

        def sweep(_, carry):
            def add(i, total):
                x = full_ref[:, columns(i)]
                return total + dot_transposed(x, x, best)

            a = lax.fori_loop(0, width // block, add, jnp.zeros((n, n), F32))
            m = coef_b * a + coef_c * jnp.dot(a, a, precision=best)

            def apply(i, carry):
                x = full_ref[:, columns(i)]
                full_ref[:, columns(i)] = coef_a * x + jnp.dot(m, x, precision=best)
                return carry

            return lax.fori_loop(0, width // block, apply, carry)

        def store(i, carry):
            put_out(columns(i), full_ref[:height, columns(i)] * scale)
            return carry

        lax.fori_loop(0, width // block, load, 0)
        lax.fori_loop(0, ITERS, sweep, 0)
        lax.fori_loop(0, width // block, store, 0)


def orthogonal(parts, count, scale):
    piece, cols = parts[0].shape
    height = piece * count
    n = sum(part.shape[0] for part in parts)
    vmem = pl.BlockSpec(memory_space=pltpu.VMEM)
    return pl.pallas_call(
        functools.partial(orthogonal_kernel, scale, count),
        in_specs=[vmem] * len(parts),
        out_specs=[vmem] * count,
        out_shape=[jax.ShapeDtypeStruct((piece, cols), BF)] * count,
        scratch_shapes=[
            pltpu.VMEM((n, cols), BF),
            pltpu.VMEM((3, n // 2, n // 2), F32),
            pltpu.VMEM((3, n // 2, n // 2), F32),
            pltpu.VMEM((height, n), F32),
            pltpu.VMEM((n, 3 * n), BF),
            pltpu.VMEM((3 * n, n), BF),
            pltpu.VMEM((3 * n, n), BF),
            pltpu.VMEM((n, 3 * n), BF),
            pltpu.VMEM((height, 3 * n), BF),
            pltpu.VMEM((n, cols), F32),
        ],
        compiler_params=pltpu.CompilerParams(vmem_limit_bytes=40 * 2**20),
        name="orthogonal",
    )(*parts)


def place_kernel(which, n_rep, *refs):
    aheads = sorted({ahead for names in which for ahead, _ in names})
    firsts = dict(zip(aheads, refs))
    parts, (*_, out_ref, sems) = refs[len(aheads) :][: len(which)], refs[len(aheads) + len(which) :]
    rows = out_ref.shape[1]
    copies = []
    for part, names in zip(parts, which):
        for i, (ahead, j) in enumerate(names):
            e = lax.rem(firsts[ahead][0] + j * n_rep, out_ref.shape[0])
            src = part.at[pl.ds(i * rows, rows)]
            copies.append(pltpu.make_async_copy(src, out_ref.at[e], sems.at[len(copies)]))
            copies[-1].start()
    for copy in copies:
        copy.wait()


def place(firsts, which, parts, n_rep, whole):
    count = sum(len(names) for names in which)
    indices = [firsts[i] for i in sorted({ahead for names in which for ahead, _ in names})]
    hbm = pl.BlockSpec(memory_space=pltpu.HBM)
    new = isinstance(whole, tuple)
    return pl.pallas_call(
        functools.partial(place_kernel, which, n_rep),
        in_specs=[pl.BlockSpec(memory_space=pltpu.SMEM)] * len(indices)
        + [pl.BlockSpec(memory_space=pl.ANY)] * len(parts)
        + [hbm] * (not new),
        out_specs=hbm,
        out_shape=jax.ShapeDtypeStruct(whole if new else whole.shape, BF),
        scratch_shapes=[pltpu.SemaphoreType.DMA((count,))],
        input_output_aliases={} if new else {len(indices) + len(parts): 0},
        cost_estimate=pl.CostEstimate(
            flops=0, bytes_accessed=4 * sum(x.size for x in parts), transcendentals=0
        ),
        compiler_params=pltpu.CompilerParams(vmem_limit_bytes=4 * 2**20),
        name="place",
    )(*indices, *parts, *([] if new else [whole]))


def solution(mesh):
    n_rep = mesh.shape["rep"]
    n_shard = mesh.shape["shard"]
    count = n_shard // n_rep
    middle = n_shard // 2
    order = [p // 2 + p % 2 * middle for p in range(n_shard)]

    def others(pieces):
        pairs = [[((i + j) % n_rep, i) for i in range(n_rep)] for j in range(1, n_rep)]
        return [[lax.ppermute(x, "rep", pair) for x in pieces] for pair in pairs]

    def exchange(pieces, there):
        moved = []
        for j, x in enumerate(pieces):
            pairs = [
                (
                    order[p] * n_rep + r,
                    order[(p + j * n_rep + r) % n_shard] * n_rep + r,
                )
                for p in range(n_shard)
                for r in range(n_rep)
            ]
            pairs = pairs if there else [pair[::-1] for pair in pairs]
            moved.append(lax.ppermute(x, ("shard", "rep"), pairs))
        return moved

    def after(x, y):
        return lax.optimization_barrier((x, y))[0]

    def shards(momentum, gradient):
        experts, rows, cols = momentum.shape
        shard, rep = lax.axis_index("shard"), lax.axis_index("rep")
        place_of = 2 * lax.rem(shard, middle) + shard // middle
        first = lax.rem(place_of + rep, n_shard)
        few = count // 4
        own = exchange(blended_share(first, momentum, gradient, count, n_rep), True)

        middle_piece = (count - 1) // 2
        momentum, gradient, own[middle_piece] = lax.optimization_barrier(
            (momentum, gradient, own[middle_piece])
        )
        new_momentum = new_momentum_of(momentum, gradient)
        own = [after(x, new_momentum) for x in own]

        scale = float(max(experts * rows, cols)) ** 0.5
        parts = own + [x for xs in others(own) for x in xs]
        update = exchange(orthogonal(parts, count, scale), False)

        firsts = [lax.rem(place_of + lax.rem(rep + i, n_rep), n_shard)[None] for i in range(n_rep)]
        early = count - few
        whole = place(
            firsts, [[(0, j)] for j in range(early)], update[:early], n_rep, (experts, rows, cols)
        )
        update[early:] = [after(x, whole) for x in update[early:]]
        pieces = {(i, j): x for i, xs in enumerate([update, *others(update)]) for j, x in enumerate(xs)}
        names = [(i, j) for i, j in pieces if i or j >= early]
        whole = place(
            firsts, [[name] for name in names], [pieces[name] for name in names], n_rep, whole
        )
        return new_momentum, whole

    return jax.shard_map(
        shards,
        mesh=mesh,
        in_specs=(P(None, "shard", None), P(None, "shard", None)),
        out_specs=(P(None, "shard", None), P(None, "shard", None)),
        check_vma=False,
    )
```

```python
import functools

import jax
import jax.numpy as jnp
from jax import lax
from jax.experimental import pallas as pl
from jax.experimental.pallas import tpu as pltpu
from jax.sharding import PartitionSpec as P

ITERS = 5

coef_a = 3.4445
coef_b = -4.775
coef_c = 2.0315

LIMIT = 4.0

BF = jnp.bfloat16
F32 = jnp.float32


def next_momentum(m, g):
    return (0.95 * m.astype(F32) + g.astype(F32)).astype(BF)


def blend(m, g):
    return (g.astype(F32) + 0.95 * next_momentum(m, g).astype(F32)).astype(BF)


def share_kernel(n_rep, at_ref, m_hbm, g_hbm, *refs):
    *share_hbms, m_ref, g_ref, share_ref, sems = refs
    count = len(share_hbms)
    experts = m_hbm.shape[0]
    copies = []
    for j in range(count):
        e = lax.rem(at_ref[0] + j * n_rep, experts)
        copies.append(
            [
                pltpu.make_async_copy(src.at[e], dst.at[j], sems.at[i, j])
                for i, (src, dst) in enumerate(((m_hbm, m_ref), (g_hbm, g_ref)))
            ]
        )
        for copy in copies[-1]:
            copy.start()
    for j, share_hbm in enumerate(share_hbms):
        for copy in copies[j]:
            copy.wait()
        share_ref[j] = blend(m_ref[j], g_ref[j])
        copies[j] = pltpu.make_async_copy(share_ref.at[j], share_hbm, sems.at[2, j])
        copies[j].start()
    for copy in copies:
        copy.wait()


def blended_share(first, momentum, gradient, count, n_rep):
    experts, rows, cols = momentum.shape
    hbm = pl.BlockSpec(memory_space=pltpu.HBM)
    return pl.pallas_call(
        functools.partial(share_kernel, n_rep),
        in_specs=[pl.BlockSpec(memory_space=pltpu.SMEM), hbm, hbm],
        out_specs=[hbm] * count,
        out_shape=[jax.ShapeDtypeStruct((rows, cols), BF)] * count,
        scratch_shapes=[pltpu.VMEM((count, rows, cols), BF)] * 3
        + [pltpu.SemaphoreType.DMA((3, count))],
        compiler_params=pltpu.CompilerParams(vmem_limit_bytes=60 * 2**20),
        name="share",
    )(first[None], momentum, gradient)


def momentum_kernel(m_ref, g_ref, new_ref):
    def one(e, carry):
        new_ref[e] = next_momentum(m_ref[e], g_ref[e])
        return carry

    lax.fori_loop(0, m_ref.shape[0], one, 0)


def new_momentum_of(momentum, gradient):
    vmem = pl.BlockSpec(memory_space=pltpu.VMEM)
    return pl.pallas_call(
        momentum_kernel,
        in_specs=[vmem, vmem],
        out_specs=vmem,
        out_shape=jax.ShapeDtypeStruct(momentum.shape, BF),
        cost_estimate=pl.CostEstimate(
            flops=2 * momentum.size, bytes_accessed=6 * momentum.size, transcendentals=0
        ),
        compiler_params=pltpu.CompilerParams(vmem_limit_bytes=16 * 2**20),
        name="new_momentum",
    )(momentum, gradient)


def halves(x):
    high = x.astype(BF)
    return high, (x - high.astype(F32)).astype(BF)


def dot(x, y):
    return jnp.dot(x, y, preferred_element_type=F32)


def dot_transposed(x, y, precision=None):
    return lax.dot_general(
        x, y, (((1,), (1,)), ((), ())), precision=precision, preferred_element_type=F32
    )


def orthogonal_kernel(scale, count, *refs):
    *parts, x_ref, a_ref, s_ref, q_ref = refs[:-6]
    parts, out_refs = parts[:-count], parts[-count:]
    a_left, a_right, m_right, s_left, q_left, full_ref = refs[-6:]
    piece, width = out_refs[0].shape
    height = count * piece
    n = x_ref.shape[0]
    half = n // 2
    at = 0
    for part in parts:
        x_ref[at : at + part.shape[0]] = part[...]
        at += part.shape[0]

    def put_out(cols, y):
        for i, out_ref in enumerate(out_refs):
            out_ref[:, cols] = y[i * piece : (i + 1) * piece].astype(BF)

    blocks = ((0, 1), (0, 0), (1, 1))

    def rows(i):
        return slice(i * half, (i + 1) * half)

    def put_left(ref, row, col, high, low):
        height, width = high.shape
        for k, part in enumerate((high, high, low)):
            ref[row : row + height, k * n + col : k * n + col + width] = part

    def put(i, j, x, left=None, right=None):
        for i, j, x in ((i, j, x), (j, i, x.T))[: 1 + (i != j)]:
            high, low = halves(x)
            if left is not None:
                put_left(left, i * half, j * half, high, low)
            if right is not None:
                for k, part in enumerate((high, low, high)):
                    right[k * n + i * half : k * n + (i + 1) * half, rows(j)] = part

    def put_q(q):
        q_ref[...] = q
        high, low = halves(q)
        put_left(q_left, 0, 0, high, low)

    def put_a(i, j, a):
        a_ref[i + j] = a
        put(i, j, a, a_left, a_right)

    eye = lax.broadcasted_iota(jnp.int32, (half, half), 0) == lax.broadcasted_iota(
        jnp.int32, (half, half), 1
    )
    gram = {(i, j): dot_transposed(x_ref[rows(i)], x_ref[rows(j)]) for i, j in blocks}
    square = jnp.sum(jnp.where(eye, gram[0, 0] + gram[1, 1], 0.0), keepdims=True)
    inverse = 1.0 / (jnp.sqrt(square) + 1e-07)
    for i, j in blocks:
        put_a(i, j, gram[i, j] * (inverse * inverse))

    for sweep in range(ITERS - 1):
        for i, j in blocks:
            m = coef_b * a_ref[i + j] + coef_c * dot(a_left[rows(i)], a_right[:, rows(j)])
            put(i, j, m, right=m_right)
            if sweep == 0 and i == 0:
                p = m + jnp.where(eye, coef_a, 0.0) if j == 0 else m
                q_ref[:, rows(j)] = p[:height]
        for i, j in blocks:
            s = coef_a * a_ref[i + j] + dot(a_left[rows(i)], m_right[:, rows(j)])
            s_ref[i + j] = s
            put(i, j, s, left=s_left)
        q = q_ref[...]
        put_q(coef_a * q + dot(q_left[...], m_right[...]) if sweep else q)
        for i, j in blocks:
            put_a(i, j, coef_a * s_ref[i + j] + dot(s_left[rows(i)], m_right[:, rows(j)]))

    q = q_ref[...]
    high, low = halves(coef_b * q + coef_c * dot(q_left[...], a_right[...]))
    put_left(s_left, 0, 0, high, low)
    q = coef_a * q + dot(s_left[:height], a_right[...])
    spread_of_values = jnp.sum(q * q) * (1.0 / (height * n))
    good = spread_of_values < LIMIT

    @pl.when(good)
    def _():
        high, low = halves(q * (inverse * scale))
        q_left[:, :n] = high
        q_left[:, n : 2 * n] = low
        block = min(width, 512)
        for at in range(0, width, block):
            x = x_ref[:, at : at + block]
            y = dot(q_left[:, :n], x) + dot(q_left[:, n : 2 * n], x)
            put_out(slice(at, at + block), y)

    @pl.when(jnp.logical_not(good))
    def _():
        best = lax.Precision.HIGHEST
        block = min(width, 512)

        def columns(i):
            return pl.ds(pl.multiple_of(i * block, block), block)

        def load(i, carry):
            full_ref[:, columns(i)] = x_ref[:, columns(i)].astype(F32) * inverse
            return carry

        def sweep(_, carry):
            def add(i, total):
                x = full_ref[:, columns(i)]
                return total + dot_transposed(x, x, best)

            a = lax.fori_loop(0, width // block, add, jnp.zeros((n, n), F32))
            m = coef_b * a + coef_c * jnp.dot(a, a, precision=best)

            def apply(i, carry):
                x = full_ref[:, columns(i)]
                full_ref[:, columns(i)] = coef_a * x + jnp.dot(m, x, precision=best)
                return carry

            return lax.fori_loop(0, width // block, apply, carry)

        def store(i, carry):
            put_out(columns(i), full_ref[:height, columns(i)] * scale)
            return carry

        lax.fori_loop(0, width // block, load, 0)
        lax.fori_loop(0, ITERS, sweep, 0)
        lax.fori_loop(0, width // block, store, 0)


def orthogonal(parts, count, scale):
    piece, cols = parts[0].shape
    height = piece * count
    n = sum(part.shape[0] for part in parts)
    vmem = pl.BlockSpec(memory_space=pltpu.VMEM)
    return pl.pallas_call(
        functools.partial(orthogonal_kernel, scale, count),
        in_specs=[vmem] * len(parts),
        out_specs=[vmem] * count,
        out_shape=[jax.ShapeDtypeStruct((piece, cols), BF)] * count,
        scratch_shapes=[
            pltpu.VMEM((n, cols), BF),
            pltpu.VMEM((3, n // 2, n // 2), F32),
            pltpu.VMEM((3, n // 2, n // 2), F32),
            pltpu.VMEM((height, n), F32),
            pltpu.VMEM((n, 3 * n), BF),
            pltpu.VMEM((3 * n, n), BF),
            pltpu.VMEM((3 * n, n), BF),
            pltpu.VMEM((n, 3 * n), BF),
            pltpu.VMEM((height, 3 * n), BF),
            pltpu.VMEM((n, cols), F32),
        ],
        compiler_params=pltpu.CompilerParams(vmem_limit_bytes=40 * 2**20),
        name="orthogonal",
    )(*parts)


def place_kernel(which, n_rep, *refs):
    aheads = sorted({ahead for names in which for ahead, _ in names})
    firsts = dict(zip(aheads, refs))
    parts, (*_, out_ref, sems) = refs[len(aheads) :][: len(which)], refs[len(aheads) + len(which) :]
    rows = out_ref.shape[1]
    copies = []
    for part, names in zip(parts, which):
        for i, (ahead, j) in enumerate(names):
            e = lax.rem(firsts[ahead][0] + j * n_rep, out_ref.shape[0])
            src = part.at[pl.ds(i * rows, rows)]
            copies.append(pltpu.make_async_copy(src, out_ref.at[e], sems.at[len(copies)]))
            copies[-1].start()
    for copy in copies:
        copy.wait()


def place(firsts, which, parts, n_rep, whole):
    count = sum(len(names) for names in which)
    indices = [firsts[i] for i in sorted({ahead for names in which for ahead, _ in names})]
    hbm = pl.BlockSpec(memory_space=pltpu.HBM)
    new = isinstance(whole, tuple)
    return pl.pallas_call(
        functools.partial(place_kernel, which, n_rep),
        in_specs=[pl.BlockSpec(memory_space=pltpu.SMEM)] * len(indices)
        + [pl.BlockSpec(memory_space=pl.ANY)] * len(parts)
        + [hbm] * (not new),
        out_specs=hbm,
        out_shape=jax.ShapeDtypeStruct(whole if new else whole.shape, BF),
        scratch_shapes=[pltpu.SemaphoreType.DMA((count,))],
        input_output_aliases={} if new else {len(indices) + len(parts): 0},
        cost_estimate=pl.CostEstimate(
            flops=0, bytes_accessed=4 * sum(x.size for x in parts), transcendentals=0
        ),
        compiler_params=pltpu.CompilerParams(vmem_limit_bytes=4 * 2**20),
        name="place",
    )(*indices, *parts, *([] if new else [whole]))


def solution(mesh):
    n_rep = mesh.shape["rep"]
    n_shard = mesh.shape["shard"]
    count = n_shard // n_rep
    middle = n_shard // 2
    order = [p // 2 + p % 2 * middle for p in range(n_shard)]

    def others(pieces):
        pairs = [[((i + j) % n_rep, i) for i in range(n_rep)] for j in range(1, n_rep)]
        return [[lax.ppermute(x, "rep", pair) for x in pieces] for pair in pairs]

    def exchange(pieces, steps, there):
        moved = []
        for j, x in zip(steps, pieces):
            pairs = [
                (
                    order[p] * n_rep + r,
                    order[(p + j * n_rep + r) % n_shard] * n_rep + r,
                )
                for p in range(n_shard)
                for r in range(n_rep)
            ]
            pairs = pairs if there else [pair[::-1] for pair in pairs]
            moved.append(lax.ppermute(x, ("shard", "rep"), pairs))
        return moved

    def after(x, y):
        return lax.optimization_barrier((x, y))[0]

    def shards(momentum, gradient):
        experts, rows, cols = momentum.shape
        shard, rep = lax.axis_index("shard"), lax.axis_index("rep")
        place_of = 2 * lax.rem(shard, middle) + shard // middle
        first = lax.rem(place_of + rep, n_shard)
        few = count // 4
        own = exchange(
            blended_share(first, momentum, gradient, count, n_rep), range(count), True
        )

        middle_piece = (count - 1) // 2
        momentum, gradient, own[middle_piece] = lax.optimization_barrier(
            (momentum, gradient, own[middle_piece])
        )
        new_momentum = new_momentum_of(momentum, gradient)
        own = [after(x, new_momentum) for x in own]

        scale = float(max(experts * rows, cols)) ** 0.5
        parts = own + [x for xs in others(own) for x in xs]
        update = orthogonal(parts, count, scale)
        early = count - few
        steps = [(j + early // 2) % early if j < early else j for j in range(count)]
        update = exchange([update[j] for j in steps], steps, False)

        firsts = [lax.rem(place_of + lax.rem(rep + i, n_rep), n_shard)[None] for i in range(n_rep)]
        whole = place(
            firsts, [[(0, j)] for j in steps[:early]], update[:early], n_rep, (experts, rows, cols)
        )
        update[early:] = [after(x, whole) for x in update[early:]]
        pieces = {(i, j): x for i, xs in enumerate([update, *others(update)]) for j, x in enumerate(xs)}
        names = [(i, j) for i, j in pieces if i or j >= early]
        whole = place(
            firsts, [[(i, steps[j])] for i, j in names], [pieces[name] for name in names], n_rep, whole
        )
        return new_momentum, whole

    return jax.shard_map(
        shards,
        mesh=mesh,
        in_specs=(P(None, "shard", None), P(None, "shard", None)),
        out_specs=(P(None, "shard", None), P(None, "shard", None)),
        check_vma=False,
    )
```

```python
import functools

import jax
import jax.numpy as jnp
from jax import lax
from jax.experimental import pallas as pl
from jax.experimental.pallas import tpu as pltpu
from jax.sharding import PartitionSpec as P

ITERS = 5

coef_a = 3.4445
coef_b = -4.775
coef_c = 2.0315

LIMIT = 4.0

BF = jnp.bfloat16
F32 = jnp.float32


def next_momentum(m, g):
    return (0.95 * m.astype(F32) + g.astype(F32)).astype(BF)


def blend(m, g):
    return (g.astype(F32) + 0.95 * next_momentum(m, g).astype(F32)).astype(BF)


def share_kernel(n_rep, at_ref, m_hbm, g_hbm, *refs):
    *share_hbms, m_ref, g_ref, share_ref, sems = refs
    count = len(share_hbms)
    experts = m_hbm.shape[0]
    copies = []
    for j in range(count):
        e = lax.rem(at_ref[0] + j * n_rep, experts)
        copies.append(
            [
                pltpu.make_async_copy(src.at[e], dst.at[j], sems.at[i, j])
                for i, (src, dst) in enumerate(((m_hbm, m_ref), (g_hbm, g_ref)))
            ]
        )
        for copy in copies[-1]:
            copy.start()
    for j, share_hbm in enumerate(share_hbms):
        for copy in copies[j]:
            copy.wait()
        share_ref[j] = blend(m_ref[j], g_ref[j])
        copies[j] = pltpu.make_async_copy(share_ref.at[j], share_hbm, sems.at[2, j])
        copies[j].start()
    for copy in copies:
        copy.wait()


def blended_share(first, momentum, gradient, count, n_rep):
    experts, rows, cols = momentum.shape
    hbm = pl.BlockSpec(memory_space=pltpu.HBM)
    return pl.pallas_call(
        functools.partial(share_kernel, n_rep),
        in_specs=[pl.BlockSpec(memory_space=pltpu.SMEM), hbm, hbm],
        out_specs=[hbm] * count,
        out_shape=[jax.ShapeDtypeStruct((rows, cols), BF)] * count,
        scratch_shapes=[pltpu.VMEM((count, rows, cols), BF)] * 3
        + [pltpu.SemaphoreType.DMA((3, count))],
        compiler_params=pltpu.CompilerParams(vmem_limit_bytes=60 * 2**20),
        name="share",
    )(first[None], momentum, gradient)


def momentum_kernel(m_ref, g_ref, new_ref):
    def one(e, carry):
        new_ref[e] = next_momentum(m_ref[e], g_ref[e])
        return carry

    lax.fori_loop(0, m_ref.shape[0], one, 0)


def new_momentum_of(momentum, gradient):
    vmem = pl.BlockSpec(memory_space=pltpu.VMEM)
    return pl.pallas_call(
        momentum_kernel,
        in_specs=[vmem, vmem],
        out_specs=vmem,
        out_shape=jax.ShapeDtypeStruct(momentum.shape, BF),
        cost_estimate=pl.CostEstimate(
            flops=2 * momentum.size, bytes_accessed=6 * momentum.size, transcendentals=0
        ),
        compiler_params=pltpu.CompilerParams(vmem_limit_bytes=16 * 2**20),
        name="new_momentum",
    )(momentum, gradient)


def halves(x):
    high = x.astype(BF)
    return high, (x - high.astype(F32)).astype(BF)


def dot(x, y):
    return jnp.dot(x, y, preferred_element_type=F32)


def dot_transposed(x, y, precision=None):
    return lax.dot_general(
        x, y, (((1,), (1,)), ((), ())), precision=precision, preferred_element_type=F32
    )


def orthogonal_kernel(scale, count, *refs):
    *parts, x_ref, a_ref, s_ref, q_ref = refs[:-6]
    parts, out_refs = parts[:-count], parts[-count:]
    a_left, a_right, m_right, s_left, q_left, full_ref = refs[-6:]
    piece, width = out_refs[0].shape
    height = count * piece
    n = x_ref.shape[0]
    half = n // 2
    at = 0
    for part in parts:
        x_ref[at : at + part.shape[0]] = part[...]
        at += part.shape[0]

    def put_out(cols, y):
        for i, out_ref in enumerate(out_refs):
            out_ref[:, cols] = y[i * piece : (i + 1) * piece].astype(BF)

    blocks = ((0, 1), (0, 0), (1, 1))

    def rows(i):
        return slice(i * half, (i + 1) * half)

    def put_left(ref, row, col, high, low):
        height, width = high.shape
        for k, part in enumerate((high, high, low)):
            ref[row : row + height, k * n + col : k * n + col + width] = part

    def put(i, j, x, left=None, right=None):
        for i, j, x in ((i, j, x), (j, i, x.T))[: 1 + (i != j)]:
            high, low = halves(x)
            if left is not None:
                put_left(left, i * half, j * half, high, low)
            if right is not None:
                for k, part in enumerate((high, low, high)):
                    right[k * n + i * half : k * n + (i + 1) * half, rows(j)] = part

    def put_q(q):
        q_ref[...] = q
        high, low = halves(q)
        put_left(q_left, 0, 0, high, low)

    def put_a(i, j, a):
        a_ref[i + j] = a
        put(i, j, a, a_left, a_right)

    eye = lax.broadcasted_iota(jnp.int32, (half, half), 0) == lax.broadcasted_iota(
        jnp.int32, (half, half), 1
    )
    gram = {(i, j): dot_transposed(x_ref[rows(i)], x_ref[rows(j)]) for i, j in blocks}
    square = jnp.sum(jnp.where(eye, gram[0, 0] + gram[1, 1], 0.0), keepdims=True)
    inverse = 1.0 / (jnp.sqrt(square) + 1e-07)
    for i, j in blocks:
        put_a(i, j, gram[i, j] * (inverse * inverse))

    for sweep in range(ITERS - 1):
        for i, j in blocks:
            m = coef_b * a_ref[i + j] + coef_c * dot(a_left[rows(i)], a_right[:, rows(j)])
            put(i, j, m, right=m_right)
            if sweep == 0 and i == 0:
                p = m + jnp.where(eye, coef_a, 0.0) if j == 0 else m
                q_ref[:, rows(j)] = p[:height]
        for i, j in blocks:
            s = coef_a * a_ref[i + j] + dot(a_left[rows(i)], m_right[:, rows(j)])
            s_ref[i + j] = s
            put(i, j, s, left=s_left)
        q = q_ref[...]
        put_q(coef_a * q + dot(q_left[...], m_right[...]) if sweep else q)
        for i, j in blocks:
            put_a(i, j, coef_a * s_ref[i + j] + dot(s_left[rows(i)], m_right[:, rows(j)]))

    q = q_ref[...]
    high, low = halves(coef_b * q + coef_c * dot(q_left[...], a_right[...]))
    put_left(s_left, 0, 0, high, low)
    q = coef_a * q + dot(s_left[:height], a_right[...])
    spread_of_values = jnp.sum(q * q) * (1.0 / (height * n))
    good = spread_of_values < LIMIT

    @pl.when(good)
    def _():
        high, low = halves(q * (inverse * scale))
        q_left[:, :n] = high
        q_left[:, n : 2 * n] = low
        block = min(width, 512)
        for at in range(0, width, block):
            x = x_ref[:, at : at + block]
            y = dot(q_left[:, :n], x) + dot(q_left[:, n : 2 * n], x)
            put_out(slice(at, at + block), y)

    @pl.when(jnp.logical_not(good))
    def _():
        best = lax.Precision.HIGHEST
        block = min(width, 512)

        def columns(i):
            return pl.ds(pl.multiple_of(i * block, block), block)

        def load(i, carry):
            full_ref[:, columns(i)] = x_ref[:, columns(i)].astype(F32) * inverse
            return carry

        def sweep(_, carry):
            def add(i, total):
                x = full_ref[:, columns(i)]
                return total + dot_transposed(x, x, best)

            a = lax.fori_loop(0, width // block, add, jnp.zeros((n, n), F32))
            m = coef_b * a + coef_c * jnp.dot(a, a, precision=best)

            def apply(i, carry):
                x = full_ref[:, columns(i)]
                full_ref[:, columns(i)] = coef_a * x + jnp.dot(m, x, precision=best)
                return carry

            return lax.fori_loop(0, width // block, apply, carry)

        def store(i, carry):
            put_out(columns(i), full_ref[:height, columns(i)] * scale)
            return carry

        lax.fori_loop(0, width // block, load, 0)
        lax.fori_loop(0, ITERS, sweep, 0)
        lax.fori_loop(0, width // block, store, 0)


def orthogonal(parts, count, scale):
    piece, cols = parts[0].shape
    height = piece * count
    n = sum(part.shape[0] for part in parts)
    vmem = pl.BlockSpec(memory_space=pltpu.VMEM)
    return pl.pallas_call(
        functools.partial(orthogonal_kernel, scale, count),
        in_specs=[vmem] * len(parts),
        out_specs=[vmem] * count,
        out_shape=[jax.ShapeDtypeStruct((piece, cols), BF)] * count,
        scratch_shapes=[
            pltpu.VMEM((n, cols), BF),
            pltpu.VMEM((3, n // 2, n // 2), F32),
            pltpu.VMEM((3, n // 2, n // 2), F32),
            pltpu.VMEM((height, n), F32),
            pltpu.VMEM((n, 3 * n), BF),
            pltpu.VMEM((3 * n, n), BF),
            pltpu.VMEM((3 * n, n), BF),
            pltpu.VMEM((n, 3 * n), BF),
            pltpu.VMEM((height, 3 * n), BF),
            pltpu.VMEM((n, cols), F32),
        ],
        compiler_params=pltpu.CompilerParams(vmem_limit_bytes=40 * 2**20),
        name="orthogonal",
    )(*parts)


def place_kernel(which, n_rep, *refs):
    aheads = sorted({ahead for names in which for ahead, _ in names})
    firsts = dict(zip(aheads, refs))
    parts, (*_, out_ref, sems) = refs[len(aheads) :][: len(which)], refs[len(aheads) + len(which) :]
    rows = out_ref.shape[1]
    copies = []
    for part, names in zip(parts, which):
        for i, (ahead, j) in enumerate(names):
            e = lax.rem(firsts[ahead][0] + j * n_rep, out_ref.shape[0])
            src = part.at[pl.ds(i * rows, rows)]
            copies.append(pltpu.make_async_copy(src, out_ref.at[e], sems.at[len(copies)]))
            copies[-1].start()
    for copy in copies:
        copy.wait()


def place(firsts, which, parts, n_rep, whole):
    count = sum(len(names) for names in which)
    indices = [firsts[i] for i in sorted({ahead for names in which for ahead, _ in names})]
    hbm = pl.BlockSpec(memory_space=pltpu.HBM)
    new = isinstance(whole, tuple)
    return pl.pallas_call(
        functools.partial(place_kernel, which, n_rep),
        in_specs=[pl.BlockSpec(memory_space=pltpu.SMEM)] * len(indices)
        + [pl.BlockSpec(memory_space=pl.ANY)] * len(parts)
        + [hbm] * (not new),
        out_specs=hbm,
        out_shape=jax.ShapeDtypeStruct(whole if new else whole.shape, BF),
        scratch_shapes=[pltpu.SemaphoreType.DMA((count,))],
        input_output_aliases={} if new else {len(indices) + len(parts): 0},
        cost_estimate=pl.CostEstimate(
            flops=0, bytes_accessed=4 * sum(x.size for x in parts), transcendentals=0
        ),
        compiler_params=pltpu.CompilerParams(vmem_limit_bytes=4 * 2**20),
        name="place",
    )(*indices, *parts, *([] if new else [whole]))


def solution(mesh):
    n_rep = mesh.shape["rep"]
    n_shard = mesh.shape["shard"]
    count = n_shard // n_rep
    middle = n_shard // 2
    order = [p // 2 + p % 2 * middle for p in range(n_shard)]

    def others(pieces):
        pairs = [[((i + j) % n_rep, i) for i in range(n_rep)] for j in range(1, n_rep)]
        return [[lax.ppermute(x, "rep", pair) for x in pieces] for pair in pairs]

    def exchange(pieces, steps, there):
        moved = []
        for j, x in zip(steps, pieces):
            pairs = [
                (
                    order[p] * n_rep + r,
                    order[(p + j * n_rep + r) % n_shard] * n_rep + r,
                )
                for p in range(n_shard)
                for r in range(n_rep)
            ]
            pairs = pairs if there else [pair[::-1] for pair in pairs]
            moved.append(lax.ppermute(x, ("shard", "rep"), pairs))
        return moved

    def after(x, y):
        return lax.optimization_barrier((x, y))[0]

    def shards(momentum, gradient):
        experts, rows, cols = momentum.shape
        shard, rep = lax.axis_index("shard"), lax.axis_index("rep")
        place_of = 2 * lax.rem(shard, middle) + shard // middle
        first = lax.rem(place_of + rep, n_shard)
        few = count // 4
        own = exchange(
            blended_share(first, momentum, gradient, count, n_rep), range(count), True
        )

        middle_piece = (count - 1) // 2
        momentum, gradient, own[middle_piece] = lax.optimization_barrier(
            (momentum, gradient, own[middle_piece])
        )
        new_momentum = new_momentum_of(momentum, gradient)
        own = [after(x, new_momentum) for x in own]

        scale = float(max(experts * rows, cols)) ** 0.5
        parts = own + [x for xs in others(own) for x in xs]
        update = orthogonal(parts, count, scale)
        early = count - few
        steps = [(j + early // 2) % early if j < early else j for j in range(count)]
        update = exchange([update[j] for j in steps], steps, False)

        firsts = [lax.rem(place_of + lax.rem(rep + i, n_rep), n_shard)[None] for i in range(n_rep)]
        whole = (experts, rows, cols)
        for i, pieces in enumerate([update, *others(update)]):
            whole = place(firsts, [[(i, j)] for j in steps], pieces, n_rep, whole)
        return new_momentum, whole

    return jax.shard_map(
        shards,
        mesh=mesh,
        in_specs=(P(None, "shard", None), P(None, "shard", None)),
        out_specs=(P(None, "shard", None), P(None, "shard", None)),
        check_vma=False,
    )
```

```python
import functools

import jax
import jax.numpy as jnp
from jax import lax
from jax.experimental import pallas as pl
from jax.experimental.pallas import tpu as pltpu
from jax.sharding import PartitionSpec as P

ITERS = 5

coef_a = 3.4445
coef_b = -4.775
coef_c = 2.0315

LIMIT = 4.0

BF = jnp.bfloat16
F32 = jnp.float32


def next_momentum(m, g):
    return (0.95 * m.astype(F32) + g.astype(F32)).astype(BF)


def blend(m, g):
    return (g.astype(F32) + 0.95 * next_momentum(m, g).astype(F32)).astype(BF)


def share_kernel(n_rep, at_ref, m_hbm, g_hbm, *refs):
    *share_hbms, m_ref, g_ref, share_ref, sems = refs
    count = len(share_hbms)
    experts = m_hbm.shape[0]
    copies = []
    for j in range(count):
        e = lax.rem(at_ref[0] + j * n_rep, experts)
        copies.append(
            [
                pltpu.make_async_copy(src.at[e], dst.at[j], sems.at[i, j])
                for i, (src, dst) in enumerate(((m_hbm, m_ref), (g_hbm, g_ref)))
            ]
        )
        for copy in copies[-1]:
            copy.start()
    for j, share_hbm in enumerate(share_hbms):
        for copy in copies[j]:
            copy.wait()
        share_ref[j] = blend(m_ref[j], g_ref[j])
        copies[j] = pltpu.make_async_copy(share_ref.at[j], share_hbm, sems.at[2, j])
        copies[j].start()
    for copy in copies:
        copy.wait()


def blended_share(first, momentum, gradient, count, n_rep):
    experts, rows, cols = momentum.shape
    hbm = pl.BlockSpec(memory_space=pltpu.HBM)
    return pl.pallas_call(
        functools.partial(share_kernel, n_rep),
        in_specs=[pl.BlockSpec(memory_space=pltpu.SMEM), hbm, hbm],
        out_specs=[hbm] * count,
        out_shape=[jax.ShapeDtypeStruct((rows, cols), BF)] * count,
        scratch_shapes=[pltpu.VMEM((count, rows, cols), BF)] * 3
        + [pltpu.SemaphoreType.DMA((3, count))],
        compiler_params=pltpu.CompilerParams(vmem_limit_bytes=62 * 2**20),
        name="share",
    )(first[None], momentum, gradient)


def momentum_kernel(m_ref, g_ref, new_ref):
    def one(e, carry):
        new_ref[e] = next_momentum(m_ref[e], g_ref[e])
        return carry

    lax.fori_loop(0, m_ref.shape[0], one, 0)


def new_momentum_of(momentum, gradient):
    vmem = pl.BlockSpec(memory_space=pltpu.VMEM)
    return pl.pallas_call(
        momentum_kernel,
        in_specs=[vmem, vmem],
        out_specs=vmem,
        out_shape=jax.ShapeDtypeStruct(momentum.shape, BF),
        cost_estimate=pl.CostEstimate(
            flops=2 * momentum.size, bytes_accessed=6 * momentum.size, transcendentals=0
        ),
        compiler_params=pltpu.CompilerParams(vmem_limit_bytes=16 * 2**20),
        name="new_momentum",
    )(momentum, gradient)


def halves(x):
    high = x.astype(BF)
    return high, (x - high.astype(F32)).astype(BF)


def dot(x, y):
    return jnp.dot(x, y, preferred_element_type=F32)


def dot_transposed(x, y, precision=None):
    return lax.dot_general(
        x, y, (((1,), (1,)), ((), ())), precision=precision, preferred_element_type=F32
    )


def orthogonal_kernel(scale, count, *refs):
    *parts, x_ref, a_ref, s_ref, q_ref = refs[:-6]
    parts, out_refs = parts[:-count], parts[-count:]
    a_left, a_right, m_right, s_left, q_left, full_ref = refs[-6:]
    piece, width = out_refs[0].shape
    height = count * piece
    n = x_ref.shape[0]
    half = n // 2
    at = 0
    for part in parts:
        x_ref[at : at + part.shape[0]] = part[...]
        at += part.shape[0]

    def put_out(cols, y):
        for i, out_ref in enumerate(out_refs):
            out_ref[:, cols] = y[i * piece : (i + 1) * piece].astype(BF)

    blocks = ((0, 1), (0, 0), (1, 1))

    def rows(i):
        return slice(i * half, (i + 1) * half)

    def put_left(ref, row, col, high, low):
        height, width = high.shape
        for k, part in enumerate((high, high, low)):
            ref[row : row + height, k * n + col : k * n + col + width] = part

    def put(i, j, x, left=None, right=None):
        for i, j, x in ((i, j, x), (j, i, x.T))[: 1 + (i != j)]:
            high, low = halves(x)
            if left is not None:
                put_left(left, i * half, j * half, high, low)
            if right is not None:
                for k, part in enumerate((high, low, high)):
                    right[k * n + i * half : k * n + (i + 1) * half, rows(j)] = part

    def put_q(q):
        q_ref[...] = q
        high, low = halves(q)
        put_left(q_left, 0, 0, high, low)

    def put_a(i, j, a):
        a_ref[i + j] = a
        put(i, j, a, a_left, a_right)

    eye = lax.broadcasted_iota(jnp.int32, (half, half), 0) == lax.broadcasted_iota(
        jnp.int32, (half, half), 1
    )
    gram = {(i, j): dot_transposed(x_ref[rows(i)], x_ref[rows(j)]) for i, j in blocks}
    square = jnp.sum(jnp.where(eye, gram[0, 0] + gram[1, 1], 0.0), keepdims=True)
    inverse = 1.0 / (jnp.sqrt(square) + 1e-07)
    for i, j in blocks:
        put_a(i, j, gram[i, j] * (inverse * inverse))

    for sweep in range(ITERS - 1):
        for i, j in blocks:
            m = coef_b * a_ref[i + j] + coef_c * dot(a_left[rows(i)], a_right[:, rows(j)])
            put(i, j, m, right=m_right)
            if sweep == 0 and i == 0:
                p = m + jnp.where(eye, coef_a, 0.0) if j == 0 else m
                q_ref[:, rows(j)] = p[:height]
        for i, j in blocks:
            s = coef_a * a_ref[i + j] + dot(a_left[rows(i)], m_right[:, rows(j)])
            s_ref[i + j] = s
            put(i, j, s, left=s_left)
        q = q_ref[...]
        put_q(coef_a * q + dot(q_left[...], m_right[...]) if sweep else q)
        for i, j in blocks:
            put_a(i, j, coef_a * s_ref[i + j] + dot(s_left[rows(i)], m_right[:, rows(j)]))

    q = q_ref[...]
    high, low = halves(coef_b * q + coef_c * dot(q_left[...], a_right[...]))
    put_left(s_left, 0, 0, high, low)
    q = coef_a * q + dot(s_left[:height], a_right[...])
    spread_of_values = jnp.sum(q * q) * (1.0 / (height * n))
    good = spread_of_values < LIMIT

    @pl.when(good)
    def _():
        high, low = halves(q * (inverse * scale))
        q_left[:, :n] = high
        q_left[:, n : 2 * n] = low
        block = min(width, 512)
        for at in range(0, width, block):
            x = x_ref[:, at : at + block]
            y = dot(q_left[:, :n], x) + dot(q_left[:, n : 2 * n], x)
            put_out(slice(at, at + block), y)

    @pl.when(jnp.logical_not(good))
    def _():
        best = lax.Precision.HIGHEST
        block = min(width, 512)

        def columns(i):
            return pl.ds(pl.multiple_of(i * block, block), block)

        def load(i, carry):
            full_ref[:, columns(i)] = x_ref[:, columns(i)].astype(F32) * inverse
            return carry

        def sweep(_, carry):
            def add(i, total):
                x = full_ref[:, columns(i)]
                return total + dot_transposed(x, x, best)

            a = lax.fori_loop(0, width // block, add, jnp.zeros((n, n), F32))
            m = coef_b * a + coef_c * jnp.dot(a, a, precision=best)

            def apply(i, carry):
                x = full_ref[:, columns(i)]
                full_ref[:, columns(i)] = coef_a * x + jnp.dot(m, x, precision=best)
                return carry

            return lax.fori_loop(0, width // block, apply, carry)

        def store(i, carry):
            put_out(columns(i), full_ref[:height, columns(i)] * scale)
            return carry

        lax.fori_loop(0, width // block, load, 0)
        lax.fori_loop(0, ITERS, sweep, 0)
        lax.fori_loop(0, width // block, store, 0)


def orthogonal(parts, count, scale):
    piece, cols = parts[0].shape
    height = piece * count
    n = sum(part.shape[0] for part in parts)
    vmem = pl.BlockSpec(memory_space=pltpu.VMEM)
    return pl.pallas_call(
        functools.partial(orthogonal_kernel, scale, count),
        in_specs=[vmem] * len(parts),
        out_specs=[vmem] * count,
        out_shape=[jax.ShapeDtypeStruct((piece, cols), BF)] * count,
        scratch_shapes=[
            pltpu.VMEM((n, cols), BF),
            pltpu.VMEM((3, n // 2, n // 2), F32),
            pltpu.VMEM((3, n // 2, n // 2), F32),
            pltpu.VMEM((height, n), F32),
            pltpu.VMEM((n, 3 * n), BF),
            pltpu.VMEM((3 * n, n), BF),
            pltpu.VMEM((3 * n, n), BF),
            pltpu.VMEM((n, 3 * n), BF),
            pltpu.VMEM((height, 3 * n), BF),
            pltpu.VMEM((n, cols), F32),
        ],
        compiler_params=pltpu.CompilerParams(vmem_limit_bytes=40 * 2**20),
        name="orthogonal",
    )(*parts)


def place_kernel(which, n_rep, *refs):
    aheads = sorted({ahead for names in which for ahead, _ in names})
    firsts = dict(zip(aheads, refs))
    parts, (*_, out_ref, sems) = refs[len(aheads) :][: len(which)], refs[len(aheads) + len(which) :]
    rows = out_ref.shape[1]
    copies = []
    for part, names in zip(parts, which):
        for i, (ahead, j) in enumerate(names):
            e = lax.rem(firsts[ahead][0] + j * n_rep, out_ref.shape[0])
            src = part.at[pl.ds(i * rows, rows)]
            copies.append(pltpu.make_async_copy(src, out_ref.at[e], sems.at[len(copies)]))
            copies[-1].start()
    for copy in copies:
        copy.wait()


def place(firsts, which, parts, n_rep, whole):
    count = sum(len(names) for names in which)
    indices = [firsts[i] for i in sorted({ahead for names in which for ahead, _ in names})]
    hbm = pl.BlockSpec(memory_space=pltpu.HBM)
    new = isinstance(whole, tuple)
    return pl.pallas_call(
        functools.partial(place_kernel, which, n_rep),
        in_specs=[pl.BlockSpec(memory_space=pltpu.SMEM)] * len(indices)
        + [pl.BlockSpec(memory_space=pl.ANY)] * len(parts)
        + [hbm] * (not new),
        out_specs=hbm,
        out_shape=jax.ShapeDtypeStruct(whole if new else whole.shape, BF),
        scratch_shapes=[pltpu.SemaphoreType.DMA((count,))],
        input_output_aliases={} if new else {len(indices) + len(parts): 0},
        cost_estimate=pl.CostEstimate(
            flops=0, bytes_accessed=4 * sum(x.size for x in parts), transcendentals=0
        ),
        compiler_params=pltpu.CompilerParams(vmem_limit_bytes=4 * 2**20),
        name="place",
    )(*indices, *parts, *([] if new else [whole]))


def solution(mesh):
    n_rep = mesh.shape["rep"]
    n_shard = mesh.shape["shard"]
    count = n_shard // n_rep
    middle = n_shard // 2
    order = [p // 2 + p % 2 * middle for p in range(n_shard)]

    def others(pieces):
        pairs = [[((i + j) % n_rep, i) for i in range(n_rep)] for j in range(1, n_rep)]
        return [[lax.ppermute(x, "rep", pair) for x in pieces] for pair in pairs]

    def exchange(pieces, steps, there):
        moved = []
        for j, x in zip(steps, pieces):
            pairs = [
                (
                    order[p] * n_rep + r,
                    order[(p + j * n_rep + r) % n_shard] * n_rep + r,
                )
                for p in range(n_shard)
                for r in range(n_rep)
            ]
            pairs = pairs if there else [pair[::-1] for pair in pairs]
            moved.append(lax.ppermute(x, ("shard", "rep"), pairs))
        return moved

    def after(x, y):
        return lax.optimization_barrier((x, y))[0]

    def shards(momentum, gradient):
        experts, rows, cols = momentum.shape
        shard, rep = lax.axis_index("shard"), lax.axis_index("rep")
        place_of = 2 * lax.rem(shard, middle) + shard // middle
        first = lax.rem(place_of + rep, n_shard)
        few = count // 4
        own = exchange(
            blended_share(first, momentum, gradient, count, n_rep), range(count), True
        )

        middle_piece = (count - 1) // 2
        momentum, gradient, own[middle_piece] = lax.optimization_barrier(
            (momentum, gradient, own[middle_piece])
        )
        new_momentum = new_momentum_of(momentum, gradient)
        own = [after(x, new_momentum) for x in own]

        scale = float(max(experts * rows, cols)) ** 0.5
        parts = own + [x for xs in others(own) for x in xs]
        update = orthogonal(parts, count, scale)
        early = count - few
        steps = [(j + early // 2) % early if j < early else j for j in range(count)]
        update = exchange([update[j] for j in steps], steps, False)

        firsts = [lax.rem(place_of + lax.rem(rep + i, n_rep), n_shard)[None] for i in range(n_rep)]
        groups = [update, *others(update)]
        names = [[(i, j)] for i in range(n_rep) for j in steps]
        pieces = [x for xs in groups for x in xs]
        whole = place(firsts, names, pieces, n_rep, (experts, rows, cols))
        return new_momentum, whole

    return jax.shard_map(
        shards,
        mesh=mesh,
        in_specs=(P(None, "shard", None), P(None, "shard", None)),
        out_specs=(P(None, "shard", None), P(None, "shard", None)),
        check_vma=False,
    )
```

```python
import functools

import jax
import jax.numpy as jnp
from jax import lax
from jax.experimental import pallas as pl
from jax.experimental.pallas import tpu as pltpu
from jax.sharding import PartitionSpec as P

ITERS = 5

coef_a = 3.4445
coef_b = -4.775
coef_c = 2.0315

LIMIT = 4.0

BF = jnp.bfloat16
F32 = jnp.float32


def next_momentum(m, g):
    return (0.95 * m.astype(F32) + g.astype(F32)).astype(BF)


def blend(m, g):
    return (g.astype(F32) + 0.95 * next_momentum(m, g).astype(F32)).astype(BF)


def share_kernel(n_rep, at_ref, m_hbm, g_hbm, *refs):
    *share_hbms, m_ref, g_ref, share_ref, sems = refs
    count = len(share_hbms)
    experts = m_hbm.shape[0]
    copies = []
    for j in range(count):
        e = lax.rem(at_ref[0] + j * n_rep, experts)
        copies.append(
            [
                pltpu.make_async_copy(src.at[e], dst.at[j], sems.at[i, j])
                for i, (src, dst) in enumerate(((m_hbm, m_ref), (g_hbm, g_ref)))
            ]
        )
        for copy in copies[-1]:
            copy.start()
    for j, share_hbm in enumerate(share_hbms):
        for copy in copies[j]:
            copy.wait()
        share_ref[j] = blend(m_ref[j], g_ref[j])
        copies[j] = pltpu.make_async_copy(share_ref.at[j], share_hbm, sems.at[2, j])
        copies[j].start()
    for copy in copies:
        copy.wait()


def blended_share(first, momentum, gradient, count, n_rep):
    experts, rows, cols = momentum.shape
    hbm = pl.BlockSpec(memory_space=pltpu.HBM)
    return pl.pallas_call(
        functools.partial(share_kernel, n_rep),
        in_specs=[pl.BlockSpec(memory_space=pltpu.SMEM), hbm, hbm],
        out_specs=[hbm] * count,
        out_shape=[jax.ShapeDtypeStruct((rows, cols), BF)] * count,
        scratch_shapes=[pltpu.VMEM((count, rows, cols), BF)] * 3
        + [pltpu.SemaphoreType.DMA((3, count))],
        compiler_params=pltpu.CompilerParams(vmem_limit_bytes=62 * 2**20),
        name="share",
    )(first[None], momentum, gradient)


def momentum_kernel(m_ref, g_ref, new_ref):
    def one(e, carry):
        new_ref[e] = next_momentum(m_ref[e], g_ref[e])
        return carry

    lax.fori_loop(0, m_ref.shape[0], one, 0)


def new_momentum_of(momentum, gradient):
    vmem = pl.BlockSpec(memory_space=pltpu.VMEM)
    return pl.pallas_call(
        momentum_kernel,
        in_specs=[vmem, vmem],
        out_specs=vmem,
        out_shape=jax.ShapeDtypeStruct(momentum.shape, BF),
        cost_estimate=pl.CostEstimate(
            flops=2 * momentum.size, bytes_accessed=6 * momentum.size, transcendentals=0
        ),
        compiler_params=pltpu.CompilerParams(vmem_limit_bytes=16 * 2**20),
        name="new_momentum",
    )(momentum, gradient)


def halves(x):
    high = x.astype(BF)
    return high, (x - high.astype(F32)).astype(BF)


def dot(x, y):
    return jnp.dot(x, y, preferred_element_type=F32)


def dot_transposed(x, y, precision=None):
    return lax.dot_general(
        x, y, (((1,), (1,)), ((), ())), precision=precision, preferred_element_type=F32
    )


def orthogonal_kernel(scale, count, *refs):
    *parts, x_ref, a_ref, s_ref, q_ref = refs[:-6]
    parts, out_refs = parts[:-count], parts[-count:]
    a_left, a_right, m_right, s_left, q_left, full_ref = refs[-6:]
    piece, width = out_refs[0].shape
    height = count * piece
    n = x_ref.shape[0]
    half = n // 2
    at = 0
    for part in parts:
        x_ref[at : at + part.shape[0]] = part[...]
        at += part.shape[0]

    def put_out(cols, y):
        for i, out_ref in enumerate(out_refs):
            out_ref[:, cols] = y[i * piece : (i + 1) * piece].astype(BF)

    blocks = ((0, 1), (0, 0), (1, 1))

    def rows(i):
        return slice(i * half, (i + 1) * half)

    def put_left(ref, row, col, high, low):
        height, width = high.shape
        for k, part in enumerate((high, high, low)):
            ref[row : row + height, k * n + col : k * n + col + width] = part

    def put(i, j, x, left=None, right=None):
        for i, j, x in ((i, j, x), (j, i, x.T))[: 1 + (i != j)]:
            high, low = halves(x)
            if left is not None:
                put_left(left, i * half, j * half, high, low)
            if right is not None:
                for k, part in enumerate((high, low, high)):
                    right[k * n + i * half : k * n + (i + 1) * half, rows(j)] = part

    def put_q(q):
        q_ref[...] = q
        high, low = halves(q)
        put_left(q_left, 0, 0, high, low)

    def put_a(i, j, a):
        a_ref[i + j] = a
        put(i, j, a, a_left, a_right)

    eye = lax.broadcasted_iota(jnp.int32, (half, half), 0) == lax.broadcasted_iota(
        jnp.int32, (half, half), 1
    )
    gram = {(i, j): dot_transposed(x_ref[rows(i)], x_ref[rows(j)]) for i, j in blocks}
    square = jnp.sum(jnp.where(eye, gram[0, 0] + gram[1, 1], 0.0), keepdims=True)
    inverse = 1.0 / (jnp.sqrt(square) + 1e-07)
    for i, j in blocks:
        put_a(i, j, gram[i, j] * (inverse * inverse))

    for sweep in range(ITERS - 1):
        for i, j in blocks:
            m = coef_b * a_ref[i + j] + coef_c * dot(a_left[rows(i)], a_right[:, rows(j)])
            put(i, j, m, right=m_right)
            if sweep == 0 and i == 0:
                p = m + jnp.where(eye, coef_a, 0.0) if j == 0 else m
                q_ref[:, rows(j)] = p[:height]
        for i, j in blocks:
            s = coef_a * a_ref[i + j] + dot(a_left[rows(i)], m_right[:, rows(j)])
            s_ref[i + j] = s
            put(i, j, s, left=s_left)
        q = q_ref[...]
        put_q(coef_a * q + dot(q_left[...], m_right[...]) if sweep else q)
        for i, j in blocks:
            put_a(i, j, coef_a * s_ref[i + j] + dot(s_left[rows(i)], m_right[:, rows(j)]))

    q = q_ref[...]
    high, low = halves(coef_b * q + coef_c * dot(q_left[...], a_right[...]))
    put_left(s_left, 0, 0, high, low)
    q = coef_a * q + dot(s_left[:height], a_right[...])
    spread_of_values = jnp.sum(q * q) * (1.0 / (height * n))
    good = spread_of_values < LIMIT

    @pl.when(good)
    def _():
        high, low = halves(q * (inverse * scale))
        q_left[:, :n] = high
        q_left[:, n : 2 * n] = low
        block = min(width, 512)
        for at in range(0, width, block):
            x = x_ref[:, at : at + block]
            y = dot(q_left[:, :n], x) + dot(q_left[:, n : 2 * n], x)
            put_out(slice(at, at + block), y)

    @pl.when(jnp.logical_not(good))
    def _():
        best = lax.Precision.HIGHEST
        block = min(width, 512)

        def columns(i):
            return pl.ds(pl.multiple_of(i * block, block), block)

        def load(i, carry):
            full_ref[:, columns(i)] = x_ref[:, columns(i)].astype(F32) * inverse
            return carry

        def sweep(_, carry):
            def add(i, total):
                x = full_ref[:, columns(i)]
                return total + dot_transposed(x, x, best)

            a = lax.fori_loop(0, width // block, add, jnp.zeros((n, n), F32))
            m = coef_b * a + coef_c * jnp.dot(a, a, precision=best)

            def apply(i, carry):
                x = full_ref[:, columns(i)]
                full_ref[:, columns(i)] = coef_a * x + jnp.dot(m, x, precision=best)
                return carry

            return lax.fori_loop(0, width // block, apply, carry)

        def store(i, carry):
            put_out(columns(i), full_ref[:height, columns(i)] * scale)
            return carry

        lax.fori_loop(0, width // block, load, 0)
        lax.fori_loop(0, ITERS, sweep, 0)
        lax.fori_loop(0, width // block, store, 0)


def orthogonal(parts, count, scale):
    piece, cols = parts[0].shape
    height = piece * count
    n = sum(part.shape[0] for part in parts)
    vmem = pl.BlockSpec(memory_space=pltpu.VMEM)
    return pl.pallas_call(
        functools.partial(orthogonal_kernel, scale, count),
        in_specs=[vmem] * len(parts),
        out_specs=[vmem] * count,
        out_shape=[jax.ShapeDtypeStruct((piece, cols), BF)] * count,
        scratch_shapes=[
            pltpu.VMEM((n, cols), BF),
            pltpu.VMEM((3, n // 2, n // 2), F32),
            pltpu.VMEM((3, n // 2, n // 2), F32),
            pltpu.VMEM((height, n), F32),
            pltpu.VMEM((n, 3 * n), BF),
            pltpu.VMEM((3 * n, n), BF),
            pltpu.VMEM((3 * n, n), BF),
            pltpu.VMEM((n, 3 * n), BF),
            pltpu.VMEM((height, 3 * n), BF),
            pltpu.VMEM((n, cols), F32),
        ],
        compiler_params=pltpu.CompilerParams(vmem_limit_bytes=40 * 2**20),
        name="orthogonal",
    )(*parts)


def place_kernel(which, n_rep, *refs):
    aheads = sorted({ahead for names in which for ahead, _ in names})
    firsts = dict(zip(aheads, refs))
    parts, (*_, out_ref, sems) = refs[len(aheads) :][: len(which)], refs[len(aheads) + len(which) :]
    rows = out_ref.shape[1]
    copies = []
    for part, names in zip(parts, which):
        for i, (ahead, j) in enumerate(names):
            e = lax.rem(firsts[ahead][0] + j * n_rep, out_ref.shape[0])
            src = part.at[pl.ds(i * rows, rows)]
            copies.append(pltpu.make_async_copy(src, out_ref.at[e], sems.at[len(copies)]))
            copies[-1].start()
    for copy in copies:
        copy.wait()


def place(firsts, which, parts, n_rep, whole):
    count = sum(len(names) for names in which)
    indices = [firsts[i] for i in sorted({ahead for names in which for ahead, _ in names})]
    hbm = pl.BlockSpec(memory_space=pltpu.HBM)
    new = isinstance(whole, tuple)
    return pl.pallas_call(
        functools.partial(place_kernel, which, n_rep),
        in_specs=[pl.BlockSpec(memory_space=pltpu.SMEM)] * len(indices)
        + [pl.BlockSpec(memory_space=pl.ANY)] * len(parts)
        + [hbm] * (not new),
        out_specs=hbm,
        out_shape=jax.ShapeDtypeStruct(whole if new else whole.shape, BF),
        scratch_shapes=[pltpu.SemaphoreType.DMA((count,))],
        input_output_aliases={} if new else {len(indices) + len(parts): 0},
        cost_estimate=pl.CostEstimate(
            flops=0, bytes_accessed=4 * sum(x.size for x in parts), transcendentals=0
        ),
        compiler_params=pltpu.CompilerParams(vmem_limit_bytes=4 * 2**20),
        name="place",
    )(*indices, *parts, *([] if new else [whole]))


def solution(mesh):
    n_rep = mesh.shape["rep"]
    n_shard = mesh.shape["shard"]
    count = n_shard // n_rep
    middle = n_shard // 2
    order = [p // 2 + p % 2 * middle for p in range(n_shard)]

    def others(pieces):
        pairs = [[((i + j) % n_rep, i) for i in range(n_rep)] for j in range(1, n_rep)]
        return [[lax.ppermute(x, "rep", pair) for x in pieces] for pair in pairs]

    def exchange(pieces, steps, there):
        moved = []
        for j, x in zip(steps, pieces):
            pairs = [
                (
                    order[p] * n_rep + r,
                    order[(p + j * n_rep + r) % n_shard] * n_rep + r,
                )
                for p in range(n_shard)
                for r in range(n_rep)
            ]
            pairs = pairs if there else [pair[::-1] for pair in pairs]
            moved.append(lax.ppermute(x, ("shard", "rep"), pairs))
        return moved

    def after(x, y):
        return lax.optimization_barrier((x, y))[0]

    def shards(momentum, gradient):
        experts, rows, cols = momentum.shape
        shard, rep = lax.axis_index("shard"), lax.axis_index("rep")
        place_of = 2 * lax.rem(shard, middle) + shard // middle
        first = lax.rem(place_of + rep, n_shard)
        few = count // 4
        early = count - few
        steps = [(j + early // 2) % early if j < early else j for j in range(count)]
        sent = blended_share(first, momentum, gradient, count, n_rep)
        own = exchange([sent[j] for j in steps], steps, True)

        middle_piece = (count - 1) // 2
        momentum, gradient, own[middle_piece] = lax.optimization_barrier(
            (momentum, gradient, own[middle_piece])
        )
        new_momentum = new_momentum_of(momentum, gradient)
        own = [after(x, new_momentum) for x in own]

        scale = float(max(experts * rows, cols)) ** 0.5
        parts = own + [x for xs in others(own) for x in xs]
        update = exchange(orthogonal(parts, count, scale), steps, False)

        firsts = [lax.rem(place_of + lax.rem(rep + i, n_rep), n_shard)[None] for i in range(n_rep)]
        groups = [update, *others(update)]
        names = [[(i, j)] for i in range(n_rep) for j in steps]
        pieces = [x for xs in groups for x in xs]
        whole = place(firsts, names, pieces, n_rep, (experts, rows, cols))
        return new_momentum, whole

    return jax.shard_map(
        shards,
        mesh=mesh,
        in_specs=(P(None, "shard", None), P(None, "shard", None)),
        out_specs=(P(None, "shard", None), P(None, "shard", None)),
        check_vma=False,
    )
```
